32 devices in a mesh: depth: 4 (over y, x), tile: 8 (over z, core).
Axes of the slice: x: 2, y: 2, z: 4, core: 2. Of those that a mesh axis runs over, the one named last changes fastest.
Arguments:
- density_blocks: bfloat16 [1024, 128, 128], P(('depth', 'tile')), may hold values from -6 to 6
- block_owner: int32 [1024], P(('depth', 'tile')), may hold values from 0 to 8, as said below
- block_place: int32 [1024], P(('depth', 'tile')), may hold values from 0 to 15, as said below
- lens_weights: float32 [16], P('depth'), may hold values from 0.02 to 0.1
- ray_cells: int32 [16, 16384], P('depth', 'tile'), may hold values from 0 to 65535
- ray_angles: float32 [2, 16384], P(None, 'tile'), may hold values from -6 to 6
Outputs:
- exit_states: float32 [4, 6, 16384], P('depth', None, 'tile')
The draws below stay inside these ranges and needn't reach their ends.
Inputs may be any that keep to these rules, and one draw needn't show every extreme that they name: `block_owner`: in every depth group each tile receives each of its 4 * 4 (plane, quadrant) places from exactly one live entry; no list sends more than 4 blocks to one tile, and in every group some list sends exactly 4 blocks to every tile. `block_place`: empty entries hold 0.
All inputs are finite; a program needn't handle non-finite values.
Results may differ from the reference program's by a relative error of at most 0.0011.
Values may be sent and summed in bfloat16 or wider, within the bound.
No kernel may reach another device: no remote copies, remote signals or barrier semaphores. Data moves between devices by JAX's collectives and lax.ppermute only.
A program may use at most 64 MiB of HBM per device.

```python
import jax
import jax.numpy as jnp
from jax import lax

TS = 256
BLK = 128
PLANES_DEV = 4
GROUPS = 4
PLANES = 16
TILES = 8
SLOTS = 32
CAP = 4
RAY_DEV = 2048
RAYS = 16384


def block_lists(key):
    base_key = jax.random.fold_in(key, 11)
    key_rank, key_jitter, key_labels, key_spots = jax.random.split(base_key, 4)
    needed = 4 * PLANES_DEV
    ranking = jax.vmap(lambda subkey: jax.random.permutation(subkey, TILES))(jax.random.split(key_rank, GROUPS))
    ranking = ranking.astype(jnp.int32)
    jitter = jax.random.randint(key_jitter, (GROUPS, TILES, TILES, CAP), 0, 64).astype(jnp.int32)
    heaviest = (ranking == TILES - 1).astype(jnp.int32) * 65536
    bonuses = ranking * 4 + heaviest
    scores = jitter + bonuses[:, None, :, None]
    flat_score = scores.reshape(GROUPS, TILES, SLOTS) * SLOTS + jnp.arange(SLOTS, dtype=jnp.int32)
    chosen = lax.top_k(flat_score, needed)[1].astype(jnp.int32)
    labels = jax.vmap(lambda subkey: jax.random.permutation(subkey, needed))(jax.random.split(key_labels, GROUPS * TILES))
    labels = labels.reshape(GROUPS, TILES, needed).astype(jnp.int32)
    matches = chosen[..., None] == jnp.arange(SLOTS, dtype=jnp.int32)
    labeled = jnp.sum(jnp.where(matches, labels[..., None] + 1, 0), axis=2).astype(jnp.int32) - 1
    labeled = labeled.reshape(GROUPS, TILES, TILES, CAP).transpose(0, 2, 1, 3).reshape(GROUPS, TILES, SLOTS)
    positions = jax.vmap(lambda subkey: jax.random.permutation(subkey, SLOTS))(jax.random.split(key_spots, GROUPS * TILES))
    positions = positions.reshape(GROUPS, TILES, SLOTS).astype(jnp.int32)
    inverse = jnp.argsort(positions, axis=-1).astype(jnp.int32)
    listed = jnp.take_along_axis(labeled, inverse, axis=-1)
    owners = jnp.where(listed >= 0, inverse // CAP, TILES).astype(jnp.int32)
    places = jnp.where(listed >= 0, listed, 0).astype(jnp.int32)
    return (owners.reshape(-1), places.reshape(-1))


def draw_block_owner(key, part):
    return block_lists(key)[0]


def draw_block_place(key, part):
    return block_lists(key)[1]


def plant(drawn, rng, least, top_value):
    longest = drawn.shape.index(max(drawn.shape))
    spots = []
    for shift in (0, 1):
        where = [jax.random.randint(jax.random.fold_in(rng, axis), (), 0, length) for axis, length in enumerate(drawn.shape)]
        where[longest] = (where[longest] + shift) % drawn.shape[longest]
        spots.append(tuple(where))
    return drawn.at[spots[0]].set(least).at[spots[1]].set(top_value)


def shard_levels(rng, shape, cuts, smallest, high):
    gain = 1.0
    for dim, parts in cuts:
        draws = jax.random.uniform(jax.random.fold_in(jax.random.fold_in(rng, 6), dim), (parts,), jnp.float32, smallest / len(cuts), high / len(cuts))
        gain = gain * jnp.repeat(jnp.exp(draws), shape[dim] // parts).reshape((-1,) + (1,) * (len(shape) - 1 - dim))
    return gain


def noise(own_key, extent, scale, reach, shards=(), kind=jnp.bfloat16):
    entries = scale * jax.random.normal(own_key, extent, jnp.float32)
    if shards:
        entries = entries * shard_levels(own_key, extent, shards, -0.22, 0.18)
    return jnp.clip(entries, -reach, reach).astype(kind)


def setup_inputs(seed: int = 0) -> dict:
    splits = jax.random.split(jax.random.key(seed), 7)
    return {
        "density_blocks": noise(splits[0], (GROUPS * TILES * SLOTS, BLK, BLK), 1.0, 6.0, ((0, 32),)),
        "block_owner": draw_block_owner(jax.random.fold_in(splits[6], 71), 0),
        "block_place": draw_block_place(jax.random.fold_in(splits[6], 71), 0),
        "lens_weights": jnp.clip(0.02 + 0.08 * jax.random.uniform(splits[3], (PLANES,), jnp.float32) ** shard_levels(splits[3], (PLANES,), ((0, 4),), -0.2, 0.2), 0.02, 0.1),
        "ray_cells": plant(jax.random.randint(splits[4], (PLANES, RAYS), 0, TS * TS), jax.random.fold_in(splits[4], 1), 0, (TS * TS) - 1).astype(jnp.int32),
        "ray_angles": noise(splits[5], (2, RAYS), 1.0, 6.0, ((1, 8),), jnp.float32),
    }


HIGHEST = lax.Precision.HIGHEST

def sine_table(length):
    index = jnp.arange(length, dtype=jnp.float32) + 1.0
    tables = jnp.sin(jnp.pi * index[:, None] * index[None, :] / (length + 1.0))
    return tables * jnp.sqrt(2.0 / (length + 1.0))

def eigen_table(length):
    index = jnp.arange(length, dtype=jnp.float32) + 1.0
    single = 2.0 - 2.0 * jnp.cos(jnp.pi * index / (length + 1.0))
    return -(single[:, None] + single[None, :])

def derive_fields(padded):
    center = padded[..., 1:-1, 1:-1]
    north = padded[..., 2:, 1:-1]
    south = padded[..., :-2, 1:-1]
    east_side = padded[..., 1:-1, 2:]
    west_side = padded[..., 1:-1, :-2]
    second_xx = north - 2.0 * center + south
    second_yy = east_side - 2.0 * center + west_side
    second_xy = 0.25 * (padded[..., 2:, 2:] - padded[..., 2:, :-2] - padded[..., :-2, 2:] + padded[..., :-2, :-2])
    return (0.5 * (north - south), 0.5 * (east_side - west_side), 0.5 * (second_xx + second_yy), 0.5 * (second_xx - second_yy), second_xy)

def reference(density_blocks, block_owner, block_place, lens_weights, ray_cells, ray_angles):
    plane_total = PLANES_DEV * GROUPS
    group_of = (jnp.arange(GROUPS * TILES * SLOTS, dtype=jnp.int32) // (TILES * SLOTS)).astype(jnp.int32)
    live_mask = block_owner < TILES
    target = ((group_of * PLANES_DEV + block_place // 4) * TILES + block_owner) * 4 + block_place % 4
    target = jnp.where(live_mask, target, plane_total * TILES * 4).astype(jnp.int32)
    layout = jnp.zeros((plane_total * TILES * 4, BLK, BLK), jnp.bfloat16).at[target].set(density_blocks, mode='drop')
    layout = layout.reshape(plane_total, TILES, 2, 2, BLK, BLK)
    tables = sine_table(TS)
    eigenvalues = eigen_table(TS)
    tile_of = (jnp.arange(RAYS, dtype=jnp.int32) // RAY_DEV).astype(jnp.int32)

    def solve_plane(operand):
        quadrants, cell_ids = operand
        convergence = quadrants.transpose(0, 1, 3, 2, 4).reshape(TILES, TS, TS).astype(jnp.float32)
        spectrum = jnp.einsum('ij,tjk,kl->til', tables, convergence, tables, precision=HIGHEST)
        potential = jnp.einsum('ij,tjk,kl->til', tables, 2.0 * spectrum / eigenvalues, tables, precision=HIGHEST)
        padded = jnp.pad(potential.reshape(TILES * TS, TS), 1)
        fields = jnp.stack(derive_fields(padded), 0).astype(jnp.bfloat16)
        row_ids = (tile_of * TS + cell_ids // TS).astype(jnp.int32)
        col_ids = (cell_ids % TS).astype(jnp.int32)
        return fields[:, row_ids, col_ids].astype(jnp.float32)
    sampled = lax.map(solve_plane, (layout, ray_cells))
    unit_row = jnp.ones((RAYS,), jnp.float32)
    zero_row = jnp.zeros((RAYS,), jnp.float32)
    initial = (unit_row, zero_row, zero_row, unit_row, ray_angles[0], ray_angles[1])

    def advance(carried, operand):
        sample_now, plane_weight = operand
        entry_xx, entry_xy, entry_yx, entry_yy, angle_x, angle_y = carried
        bend_x, bend_y, convergence, shear_one, shear_two = sample_now
        upper_diag = convergence + shear_one
        lower_diag = convergence - shear_one
        updated = (entry_xx - plane_weight * (upper_diag * entry_xx + shear_two * entry_yx), entry_xy - plane_weight * (upper_diag * entry_xy + shear_two * entry_yy), entry_yx - plane_weight * (shear_two * entry_xx + lower_diag * entry_yx), entry_yy - plane_weight * (shear_two * entry_xy + lower_diag * entry_yy), angle_x - plane_weight * bend_x, angle_y - plane_weight * bend_y)
        return (updated, jnp.stack(updated, 0))
    final_state, history = lax.scan(advance, initial, (sampled, lens_weights))
    return history[PLANES_DEV - 1::PLANES_DEV]
```

```python
import functools

import jax
import jax.numpy as jnp
import ml_dtypes
import numpy as np
from jax import lax
from jax.experimental import pallas as pl
from jax.experimental.pallas import tpu as pltpu
from jax.sharding import PartitionSpec as P

F32 = jnp.float32
BF16 = jnp.bfloat16
LANES = 128
VMEM = pl.BlockSpec(memory_space=pltpu.VMEM)
SMEM = pl.BlockSpec(memory_space=pltpu.SMEM)


def call(kernel, outs, in_specs, scratch=(), limit=48, flops=0, moved=0):
    return pl.pallas_call(
        kernel,
        out_shape=outs,
        in_specs=in_specs,
        out_specs=jax.tree.map(lambda _: VMEM, outs),
        scratch_shapes=list(scratch),
        compiler_params=pltpu.CompilerParams(vmem_limit_bytes=limit << 20),
        cost_estimate=pl.CostEstimate(flops=flops, bytes_accessed=moved, transcendentals=0),
    )


def mul(a, b):
    return jnp.dot(a, b, preferred_element_type=F32)


def halves(a):
    high = a.astype(BF16)
    return high, (a - high.astype(F32)).astype(BF16)


def label_rows(capacity):
    return -(-capacity // 16) * 16


def tables(side):
    index = np.arange(side, dtype=np.float64) + 1.0
    sines = np.sqrt(2.0 / (side + 1.0)) * np.sin(np.pi * index[:, None] * index[None, :] / (side + 1.0))
    high = sines.astype(np.float32).astype(ml_dtypes.bfloat16)
    low = (sines - high.astype(np.float64)).astype(np.float32).astype(ml_dtypes.bfloat16)
    single = 2.0 - 2.0 * np.cos(np.pi * index / (side + 1.0))
    inverse = -2.0 / (single[:, None] + single[None, :])
    across = np.concatenate([high, high, low], axis=1)
    down = np.concatenate([high, high, low], axis=0)
    return across, down, np.concatenate([high, low], axis=0), inverse.astype(np.float32)


def pack_kernel(tile_count, capacity, tile_ref, owner_ref, place_ref, blocks_ref, *rest):
    outs, slot_ref, count_ref = rest[:tile_count], rest[-2], rest[-1]
    slots, side = blocks_ref.shape[0], blocks_ref.shape[1]
    spare = tile_count * capacity
    tile = tile_ref[0]
    for x in range(tile_count + 1):
        count_ref[x] = 0
    for i in range(spare):
        slot_ref[i] = -1
    for e in range(slots):
        owner = owner_ref[e]
        live = owner < tile_count
        chunk = jnp.where(live, owner ^ tile, tile_count)
        count = count_ref[chunk]
        count_ref[chunk] = count + 1
        slot_ref[jnp.where(live, chunk * capacity + count, spare + e)] = e
    rows = label_rows(capacity)
    row = lax.broadcasted_iota(jnp.int32, (rows, side), 0)
    for x in range(tile_count):
        labels = jnp.full((rows, side), -1, jnp.int32)
        for c in range(capacity):
            entry = slot_ref[x * capacity + c]
            safe = jnp.maximum(entry, 0)
            label = jnp.where(entry >= 0, place_ref[safe], -1)
            outs[x][pl.ds(c * side, side), :] = blocks_ref[safe]
            labels = jnp.where(row == c, label, labels)
        outs[x][pl.ds(capacity * side, rows), :] = labels.astype(F32).astype(BF16)


def solve_kernel(capacity, planes, *refs):
    across_ref, down_ref, pair_ref, inverse_ref = refs[:4]
    chunks, (p_ref, c_ref, edge_ref) = refs[4:-3], refs[-3:]
    side = chunks[0].shape[1]
    c_ref[...] = jnp.zeros(c_ref.shape, BF16)
    rows = label_rows(capacity)
    for chunk in chunks:
        labels = chunk[pl.ds(capacity * side, rows), :].astype(F32).astype(jnp.int32)
        for c in range(capacity):
            label = labels[c, 0]

            @pl.when(label >= 0)
            def _():
                top = pl.multiple_of(((label >> 1) & 1) * side, side)
                left = pl.multiple_of((label & 1) * side, side)
                c_ref[label >> 2, pl.ds(top, side), pl.ds(left, side)] = chunk[pl.ds(c * side, side), :]

    across, down, pair, inverse = across_ref[...], down_ref[...], pair_ref[...], inverse_ref[...]
    for k in range(planes):
        mass = c_ref[k]
        half = mul(jnp.concatenate([mass, mass], axis=1), pair)
        high, low = halves(half)
        spectrum = mul(across, jnp.concatenate([high, low, high], axis=0)) * inverse
        high, low = halves(spectrum)
        half = mul(jnp.concatenate([high, low, high], axis=1), down)
        high, low = halves(half)
        potential = mul(across, jnp.concatenate([high, low, high], axis=0))
        p_ref[k] = potential
        edge_ref[pl.ds(k, 1), :] = potential[:1]
        edge_ref[pl.ds(planes + k, 1), :] = potential[2 * side - 1 :]


def shifted(a, axis, step):
    size = a.shape[axis]
    place = lax.broadcasted_iota(jnp.int32, a.shape, axis)
    edge = size - 1 if step > 0 else 0
    return jnp.where(place == edge, 0.0, pltpu.roll(a, (-step) % size, axis))


def pick_kernel(planes, p_ref, c_ref, cells_ref, out_ref):
    side = p_ref.shape[1]
    shift = side.bit_length() - 1
    groups = cells_ref.shape[0] // planes
    width = 2 if groups % 2 == 0 else 1
    sub = lax.broadcasted_iota(jnp.int32, (8, width * LANES), 0)
    column = lax.broadcasted_iota(jnp.int32, (side, width * LANES), 0)
    for k in range(planes):
        p = p_ref[k]
        above, below = shifted(p, 0, -1), shifted(p, 0, 1)
        left, right = shifted(p, 1, -1), shifted(p, 1, 1)
        slope = 0.5 * (below - above)
        fields = (
            slope.astype(BF16),
            (0.5 * (right - left)).astype(BF16),
            c_ref[k],
            (0.5 * ((below + above) - (right + left))).astype(BF16),
            (0.5 * (shifted(slope, 1, 1) - shifted(slope, 1, -1))).astype(BF16),
        )
        for g in range(0, groups, width):
            cells = jnp.concatenate([cells_ref[pl.ds(k * groups + g + w, 1), :] for w in range(width)], axis=1)
            row, col = cells >> shift, cells & (side - 1)
            chosen = (column == col).astype(F32).astype(BF16)
            block, within = row >> 3, sub == (row & 7)
            for f in range(5):
                picked = mul(fields[f], chosen)
                kept = picked[:8]
                for v in range(1, side // 8):
                    kept = jnp.where(block == v, picked[v * 8 : v * 8 + 8], kept)
                value = jnp.sum(jnp.where(within, kept, 0.0), axis=0, keepdims=True)
                for w in range(width):
                    out_ref[pl.ds((k * 5 + f) * groups + g + w, 1), :] = value[:, w * LANES : (w + 1) * LANES]


def taken(table, index):
    parts = table.shape[1] // LANES
    rows = index.shape[0]
    lane, part = index & (LANES - 1), index >> 7
    out = None
    for i in range(parts):
        spread = jnp.broadcast_to(table[:, i * LANES : (i + 1) * LANES], (rows, LANES))
        got = jnp.take_along_axis(spread, lane, axis=1, mode="promise_in_bounds")
        out = got if out is None else jnp.where(part == i, got, out)
    return out


def combine_kernel(planes, side, tile_ref, weights_ref, one_ref, two_ref, cells_ref, first_ref, second_ref, out_ref):
    groups = cells_ref.shape[0] // planes
    shift = side.bit_length() - 1
    even = (tile_ref[0] & 1) == 0
    axx = ayy = jnp.ones((groups, LANES), F32)
    axy = ayx = bx = by = jnp.zeros((groups, LANES), F32)
    for k in range(planes):
        cells = cells_ref[pl.ds(k * groups, groups), :]
        row, col = cells >> shift, cells & (side - 1)
        first, second = first_ref[pl.ds(k, 1), :], second_ref[pl.ds(k, 1), :]
        above, below = jnp.where(even, second, first), jnp.where(even, first, second)
        at_top, at_end = row == 0, row == side - 1
        up, down = taken(above, col), taken(below, col)
        up_x = taken(shifted(above, 1, 1) - shifted(above, 1, -1), col)
        down_x = taken(shifted(below, 1, 1) - shifted(below, 1, -1), col)
        near = jnp.where(at_top, up, 0.0)
        far = jnp.where(at_end, down, 0.0)
        cross = 0.25 * (jnp.where(at_end, down_x, 0.0) - jnp.where(at_top, up_x, 0.0))

        def read(f):
            at = pl.ds((k * 5 + f) * groups, groups)
            return one_ref[at, :] + two_ref[at, :]

        weight = weights_ref[k]
        bend_x, bend_y = read(0) + 0.5 * (far - near), read(1)
        extra = 0.5 * (far + near)
        kappa, shear, mixed = read(2) + extra, read(3) + extra, read(4) + cross
        upper, lower = weight * (kappa + shear), weight * (kappa - shear)
        mixed = weight * mixed
        axx, ayx = axx - (upper * axx + mixed * ayx), ayx - (mixed * axx + lower * ayx)
        axy, ayy = axy - (upper * axy + mixed * ayy), ayy - (mixed * axy + lower * ayy)
        bx, by = bx - weight * bend_x, by - weight * bend_y
    for i, value in enumerate((axx, axy, ayx, ayy, bx, by)):
        out_ref[pl.ds(i * groups, groups), :] = value


def compose_kernel(depth_ref, maps_ref, angles_ref, out_ref):
    count = maps_ref.shape[0]
    groups = maps_ref.shape[1] // 6
    depth = depth_ref[0]

    def part(d, i):
        return maps_ref[d, pl.ds(i * groups, groups), :]

    xx, xy, yx, yy, bx, by = (part(0, i) for i in range(6))
    for d in range(1, count):
        used = d <= depth
        mxx, mxy, myx, myy, mbx, mby = (part(d, i) for i in range(6))
        nxx, nxy = mxx * xx + mxy * yx, mxx * xy + mxy * yy
        nyx, nyy = myx * xx + myy * yx, myx * xy + myy * yy
        new = (nxx, nxy, nyx, nyy, bx + mbx, by + mby)
        xx, xy, yx, yy, bx, by = (jnp.where(used, a, b) for a, b in zip(new, (xx, xy, yx, yy, bx, by)))
    bx = bx + angles_ref[pl.ds(0, groups), :]
    by = by + angles_ref[pl.ds(groups, groups), :]
    for i, value in enumerate((xx, xy, yx, yy, bx, by)):
        for g in range(groups):
            out_ref[0, pl.ds(i, 1), pl.ds(g * LANES, LANES)] = value[g : g + 1]


def body(density_blocks, block_owner, block_place, lens_weights, ray_cells, ray_angles):
    slots, block_side = density_blocks.shape[:2]
    side = 2 * block_side
    planes, rays = ray_cells.shape
    groups = rays // LANES
    tile_count = lax.axis_size("tile")
    capacity = slots // tile_count
    half = tile_count // 2
    tile = lax.axis_index("tile").astype(jnp.int32).reshape(1)
    depth = lax.axis_index("depth").astype(jnp.int32).reshape(1)
    across, down, pair, inverse = (jnp.asarray(t) for t in tables(side))
    cells = ray_cells.reshape(planes * groups, LANES)
    angles = ray_angles.reshape(2 * groups, LANES)

    def swap(array, bits):
        return lax.ppermute(array, "tile", [(i, i ^ bits) for i in range(tile_count)])

    rows = capacity * block_side + label_rows(capacity)
    chunks = call(
        functools.partial(pack_kernel, tile_count, capacity),
        [jax.ShapeDtypeStruct((rows, block_side), BF16)] * tile_count,
        [SMEM, SMEM, SMEM, VMEM],
        [pltpu.SMEM((tile_count * capacity + slots,), jnp.int32), pltpu.SMEM((tile_count + 1,), jnp.int32)],
        moved=2 * density_blocks.size * 2,
    )(tile, block_owner, block_place, density_blocks)
    order = list(range(2, half)) + [1] if half > 1 else []
    theirs = [chunks[half]] + [swap(chunks[s + half], s) for s in order]
    ours = [chunks[0]] + [swap(chunks[s], s) for s in order]
    their_cells = swap(cells, half)

    def solve(received):
        return call(
            functools.partial(solve_kernel, capacity, planes),
            [
                jax.ShapeDtypeStruct((planes, side, side), F32),
                jax.ShapeDtypeStruct((planes, side, side), BF16),
                jax.ShapeDtypeStruct((2 * planes, side), F32),
            ],
            [VMEM] * (4 + half),
            flops=2 * 11 * planes * side**3,
        )(across, down, pair, inverse, *received)

    def pick(potential, mass, at):
        return call(
            functools.partial(pick_kernel, planes),
            [jax.ShapeDtypeStruct((planes * 5 * groups, LANES), F32)],
            [VMEM] * 3,
            flops=2 * 5 * planes * side * side * rays,
        )(potential, mass, at)[0]

    potential, mass, their_edges = solve(theirs)
    other_edges = swap(their_edges, half)
    other_samples = swap(pick(potential, mass, their_cells), half)
    potential, mass, our_edges = solve(ours)
    edges = our_edges + other_edges
    even = tile[0] % 2 == 0
    top, end = edges[:planes], edges[planes:]
    first = swap(jnp.where(even, end, top), 1)
    pairs = [(i, i + 1) for i in range(1, tile_count - 1, 2)]
    second = lax.ppermute(jnp.where(even, top, end), "tile", pairs + [(j, i) for i, j in pairs])
    own_samples = pick(potential, mass, cells)
    local_map = call(
        functools.partial(combine_kernel, planes, side),
        [jax.ShapeDtypeStruct((6 * groups, LANES), F32)],
        [SMEM, SMEM, VMEM, VMEM, VMEM, VMEM, VMEM],
    )(tile, lens_weights, own_samples, other_samples, cells, first, second)[0]
    maps = lax.all_gather(local_map, "depth")
    return call(
        compose_kernel,
        [jax.ShapeDtypeStruct((1, 6, rays), F32)],
        [SMEM, VMEM, VMEM],
    )(depth, maps, angles)[0]


def solution(mesh):
    return jax.shard_map(
        body,
        mesh=mesh,
        in_specs=(
            P(("depth", "tile"), None, None),
            P(("depth", "tile")),
            P(("depth", "tile")),
            P("depth"),
            P("depth", "tile"),
            P(None, "tile"),
        ),
        out_specs=P("depth", None, "tile"),
        check_vma=False,
    )
```

```python
import functools

import jax
import jax.numpy as jnp
import ml_dtypes
import numpy as np
from jax import lax
from jax.experimental import pallas as pl
from jax.experimental.pallas import tpu as pltpu
from jax.sharding import PartitionSpec as P

F32 = jnp.float32
BF16 = jnp.bfloat16
LANES = 128
VMEM = pl.BlockSpec(memory_space=pltpu.VMEM)
SMEM = pl.BlockSpec(memory_space=pltpu.SMEM)
HBM = pl.BlockSpec(memory_space=pltpu.HBM)


def call(kernel, outs, in_specs, scratch=(), limit=48, flops=0, moved=0):
    return pl.pallas_call(
        kernel,
        out_shape=outs,
        in_specs=in_specs,
        out_specs=jax.tree.map(lambda _: VMEM, outs),
        scratch_shapes=list(scratch),
        compiler_params=pltpu.CompilerParams(vmem_limit_bytes=limit << 20),
        cost_estimate=pl.CostEstimate(flops=flops, bytes_accessed=moved, transcendentals=0),
    )


def mul(a, b):
    return jnp.dot(a, b, preferred_element_type=F32)


def halves(a):
    high = a.astype(BF16)
    return high, (a - high.astype(F32)).astype(BF16)


def label_rows(capacity):
    return -(-capacity // 16) * 16


def tables(side):
    index = np.arange(side, dtype=np.float64) + 1.0
    sines = np.sqrt(2.0 / (side + 1.0)) * np.sin(np.pi * index[:, None] * index[None, :] / (side + 1.0))
    high = sines.astype(np.float32).astype(ml_dtypes.bfloat16)
    low = (sines - high.astype(np.float64)).astype(np.float32).astype(ml_dtypes.bfloat16)
    single = 2.0 - 2.0 * np.cos(np.pi * index / (side + 1.0))
    inverse = -2.0 / (single[:, None] + single[None, :])
    return high, low, inverse.astype(np.float32)


def pack_kernel(tile_count, capacity, layout, tile_ref, owner_ref, place_ref, blocks_ref, *rest):
    outs, slot_ref, count_ref = rest[-2 - len(layout) : -2], rest[-2], rest[-1]
    slots, side = blocks_ref.shape[0], blocks_ref.shape[1]
    spare = tile_count * capacity
    tile = tile_ref[0]
    for x in range(tile_count + 1):
        count_ref[x] = 0
    for i in range(spare):
        slot_ref[i] = -1
    for e in range(slots):
        owner = owner_ref[e]
        live = owner < tile_count
        chunk = jnp.where(live, owner ^ tile, tile_count)
        count = count_ref[chunk]
        count_ref[chunk] = count + 1
        slot_ref[jnp.where(live, chunk * capacity + count, spare + e)] = e
    rows = label_rows(capacity)
    row = lax.broadcasted_iota(jnp.int32, (rows, side), 0)
    for out, members in zip(outs, layout):
        for i, x in enumerate(members):
            base = i * (capacity * side + rows)
            labels = jnp.full((rows, side), -1, jnp.int32)
            for c in range(capacity):
                entry = slot_ref[x * capacity + c]
                safe = jnp.maximum(entry, 0)
                label = jnp.where(entry >= 0, place_ref[safe], -1)
                out[pl.ds(base + c * side, side), :] = blocks_ref[safe]
                labels = jnp.where(row == c, label, labels)
            out[pl.ds(base + capacity * side, rows), :] = labels.astype(F32).astype(BF16)


def solve_kernel(capacity, planes, *refs):
    high_ref, low_ref, inverse_ref = refs[:3]
    chunks, (p_ref, c_ref, edge_ref) = refs[3:-3], refs[-3:]
    side = chunks[0].shape[1]
    c_ref[...] = jnp.zeros(c_ref.shape, BF16)
    rows = label_rows(capacity)
    for chunk in chunks:
        labels = chunk[pl.ds(capacity * side, rows), :].astype(F32).astype(jnp.int32)
        for c in range(capacity):
            label = labels[c, 0]

            @pl.when(label >= 0)
            def _():
                top = pl.multiple_of(((label >> 1) & 1) * side, side)
                left = pl.multiple_of((label & 1) * side, side)
                c_ref[label >> 2, pl.ds(top, side), pl.ds(left, side)] = chunk[pl.ds(c * side, side), :]

    high, low, inverse = high_ref[...], low_ref[...], inverse_ref[...]
    across = jnp.concatenate([high, high, low], axis=1)
    down = jnp.concatenate([high, high, low], axis=0)
    pair = jnp.concatenate([high, low], axis=0)

    def right(a, b):
        return mul(jnp.concatenate([a, b, a], axis=1), down)

    def left(a, b):
        return mul(across, jnp.concatenate([a, b, a], axis=0))

    mass = [c_ref[k] for k in range(planes)]
    parts = [halves(mul(jnp.concatenate([m, m], axis=1), pair)) for m in mass]
    parts = [halves(left(*part) * inverse) for part in parts]
    parts = [halves(right(*part)) for part in parts]
    for k in range(planes):
        potential = left(*parts[k])
        p_ref[k] = potential
        edge_ref[pl.ds(k, 1), :] = potential[:1]
        edge_ref[pl.ds(planes + k, 1), :] = potential[2 * side - 1 :]


def shifted(a, axis, step):
    size = a.shape[axis]
    tile = 8 if axis == 0 and size > 8 else min(size, LANES)
    rolled = pltpu.roll(a, (-step) % size, axis)
    at = size - tile if step > 0 else 0
    last = lax.slice_in_dim(rolled, at, at + tile, axis=axis)
    place = lax.broadcasted_iota(jnp.int32, last.shape, axis)
    last = jnp.where(place == (tile - 1 if step > 0 else 0), 0.0, last)
    if size == tile:
        return last
    if step > 0:
        return jnp.concatenate([lax.slice_in_dim(rolled, 0, at, axis=axis), last], axis=axis)
    return jnp.concatenate([last, lax.slice_in_dim(rolled, tile, size, axis=axis)], axis=axis)


def pick_kernel(planes, p_ref, c_ref, cells_ref, last_ref, out_ref):
    side = p_ref.shape[1]
    shift = side.bit_length() - 1
    groups = cells_ref.shape[0] // planes
    width = 2 if groups % 2 == 0 else 1
    sub = lax.broadcasted_iota(jnp.int32, (8, width * LANES), 0)
    column = lax.broadcasted_iota(jnp.int32, (side, width * LANES), 0)
    for k in range(planes):
        p = p_ref[k]
        above, below = shifted(p, 0, -1), shifted(p, 0, 1)
        left, right = shifted(p, 1, -1), shifted(p, 1, 1)
        tilt = 0.5 * (right - left)
        fields = (
            (0.5 * (below - above)).astype(BF16),
            tilt.astype(BF16),
            c_ref[k],
            (0.5 * ((below + above) - (right + left))).astype(BF16),
            (0.5 * (shifted(tilt, 0, 1) - shifted(tilt, 0, -1))).astype(BF16),
        )
        for g in range(0, groups, width):
            cells = jnp.concatenate([cells_ref[pl.ds(k * groups + g + w, 1), :] for w in range(width)], axis=1)
            row, col = cells >> shift, cells & (side - 1)
            chosen = (column == col).astype(F32).astype(BF16)
            block, within = row >> 3, sub == (row & 7)
            bits = [(block >> i) & 1 == 1 for i in range((side // 8).bit_length() - 1)]
            for f in range(5):
                picked = mul(fields[f], chosen)
                kept = [picked[v * 8 : v * 8 + 8] for v in range(side // 8)]
                for bit in bits:
                    kept = [jnp.where(bit, b, a) for a, b in zip(kept[::2], kept[1::2])]
                value = jnp.sum(jnp.where(within, kept[0], 0.0), axis=0, keepdims=True)
                for w in range(width):
                    out_ref[pl.ds((k * 5 + f) * groups + g + w, 1), :] = value[:, w * LANES : (w + 1) * LANES]
    last_ref[...] = out_ref[...].astype(last_ref.dtype)


def taken(table, index):
    parts = table.shape[1] // LANES
    rows = index.shape[0]
    lane, part = index & (LANES - 1), index >> 7
    out = None
    for i in range(parts):
        spread = jnp.broadcast_to(table[:, i * LANES : (i + 1) * LANES], (rows, LANES))
        got = jnp.take_along_axis(spread, lane, axis=1, mode="promise_in_bounds")
        out = got if out is None else jnp.where(part == i, got, out)
    return out


def combine_kernel(tile_count, planes, side, tile_ref, weights_ref, one_ref, two_ref, cells_ref, first_ref, second_ref, out_ref):
    groups = cells_ref.shape[0] // planes
    shift = side.bit_length() - 1
    tile = tile_ref[0]
    even = (tile & 1) == 0
    starts, ends = tile == 0, tile == tile_count - 1
    axx = ayy = jnp.ones((groups, LANES), F32)
    axy = ayx = bx = by = jnp.zeros((groups, LANES), F32)
    for k in range(planes):
        cells = cells_ref[pl.ds(k * groups, groups), :]
        row, col = cells >> shift, cells & (side - 1)
        first, second = first_ref[pl.ds(k, 1), :], second_ref[pl.ds(k, 1), :]
        above, below = jnp.where(even, second, first), jnp.where(even, first, second)
        above, below = jnp.where(starts, 0.0, above), jnp.where(ends, 0.0, below)
        at_top, at_end = row == 0, row == side - 1
        up, down = taken(above, col), taken(below, col)
        up_x = taken(shifted(above, 1, 1) - shifted(above, 1, -1), col)
        down_x = taken(shifted(below, 1, 1) - shifted(below, 1, -1), col)
        near = jnp.where(at_top, up, 0.0)
        far = jnp.where(at_end, down, 0.0)
        cross = 0.25 * (jnp.where(at_end, down_x, 0.0) - jnp.where(at_top, up_x, 0.0))

        def read(f):
            at = pl.ds((k * 5 + f) * groups, groups)
            return one_ref[at, :] + two_ref[at, :].astype(F32)

        weight = weights_ref[k]
        bend_x, bend_y = read(0) + 0.5 * (far - near), read(1)
        extra = 0.5 * (far + near)
        kappa, shear, mixed = read(2) + extra, read(3) + extra, read(4) + cross
        upper, lower = weight * (kappa + shear), weight * (kappa - shear)
        mixed = weight * mixed
        axx, ayx = axx - (upper * axx + mixed * ayx), ayx - (mixed * axx + lower * ayx)
        axy, ayy = axy - (upper * axy + mixed * ayy), ayy - (mixed * axy + lower * ayy)
        bx, by = bx - weight * bend_x, by - weight * bend_y
    for i, value in enumerate((axx, axy, ayx, ayy, bx, by)):
        out_ref[pl.ds(i * groups, groups), :] = value


def compose_kernel(depth_ref, maps_ref, angles_ref, out_ref):
    count = maps_ref.shape[0]
    groups = maps_ref.shape[1] // 6
    depth = depth_ref[0]

    def part(d, i):
        return maps_ref[d, pl.ds(i * groups, groups), :]

    xx, xy, yx, yy, bx, by = (part(0, i) for i in range(6))
    for d in range(1, count):
        used = d <= depth
        mxx, mxy, myx, myy, mbx, mby = (part(d, i) for i in range(6))
        nxx, nxy = mxx * xx + mxy * yx, mxx * xy + mxy * yy
        nyx, nyy = myx * xx + myy * yx, myx * xy + myy * yy
        new = (nxx, nxy, nyx, nyy, bx + mbx, by + mby)
        xx, xy, yx, yy, bx, by = (jnp.where(used, a, b) for a, b in zip(new, (xx, xy, yx, yy, bx, by)))
    bx = bx + angles_ref[pl.ds(0, groups), :]
    by = by + angles_ref[pl.ds(groups, groups), :]
    for i, value in enumerate((xx, xy, yx, yy, bx, by)):
        out_ref[pl.ds(i * groups, groups), :] = value


def body(density_blocks, block_owner, block_place, lens_weights, ray_cells, ray_angles):
    slots, block_side = density_blocks.shape[:2]
    side = 2 * block_side
    planes, rays = ray_cells.shape
    groups = rays // LANES
    tile_count = lax.axis_size("tile")
    capacity = slots // tile_count
    half = tile_count // 2
    tile = lax.axis_index("tile").astype(jnp.int32).reshape(1)
    depth = lax.axis_index("depth").astype(jnp.int32).reshape(1)
    high, low, inverse = (jnp.asarray(t) for t in tables(side))
    cells = ray_cells.reshape(planes * groups, LANES)
    angles = ray_angles.reshape(2 * groups, LANES)

    def swap(array, bits):
        return lax.ppermute(array, "tile", [(i, i ^ bits) for i in range(tile_count)])

    rows = capacity * block_side + label_rows(capacity)
    order = list(range(2, half)) + [1]
    layout = [[half + x] for x in order] + [[half]] + [[x] for x in order] + [[0]]
    packed = call(
        functools.partial(pack_kernel, tile_count, capacity, layout),
        [jax.ShapeDtypeStruct((rows, block_side), BF16)] * tile_count,
        [SMEM, SMEM, SMEM, VMEM],
        [pltpu.SMEM((tile_count * capacity + slots,), jnp.int32), pltpu.SMEM((tile_count + 1,), jnp.int32)],
        moved=2 * density_blocks.size,
    )(tile, block_owner, block_place, density_blocks)
    theirs = [swap(chunk, x) for x, chunk in zip(order, packed)] + [packed[half - 1]]
    ours = [swap(chunk, x) for x, chunk in zip(order, packed[half:])] + [packed[-1]]
    their_cells = swap(cells, half)

    def solve(arrays):
        return call(
            functools.partial(solve_kernel, capacity, planes),
            [
                jax.ShapeDtypeStruct((planes, side, side), F32),
                jax.ShapeDtypeStruct((planes, side, side), BF16),
                jax.ShapeDtypeStruct((2 * planes, side), F32),
            ],
            [VMEM] * (3 + len(arrays)),
        )(high, low, inverse, *arrays)

    def pick(potential, mass, at, dtype):
        shape = (planes * 5 * groups, LANES)
        return call(
            functools.partial(pick_kernel, planes),
            [jax.ShapeDtypeStruct(shape, dtype)],
            [VMEM] * 3,
            [pltpu.VMEM(shape, F32)],
            flops=2 * 5 * planes * side * side * rays,
        )(potential, mass, at)[0]

    potential, mass, their_edges = solve(theirs)
    samples, their_edges = lax.optimization_barrier((pick(potential, mass, their_cells, BF16), their_edges))
    other_edges, other_samples = swap(their_edges, half), swap(samples, half)
    potential, mass, our_edges = solve(ours)
    edges = our_edges + other_edges
    even = tile[0] % 2 == 0
    top, end = edges[:planes], edges[planes:]
    first = swap(jnp.where(even, end, top), 1)
    pairs = [(i, (i + 1) % tile_count) for i in range(1, tile_count, 2)]
    second = lax.ppermute(jnp.where(even, top, end), "tile", pairs + [(j, i) for i, j in pairs])
    own_samples = pick(potential, mass, cells, F32)
    local_map = call(
        functools.partial(combine_kernel, tile_count, planes, side),
        [jax.ShapeDtypeStruct((6 * groups, LANES), F32)],
        [SMEM, SMEM, VMEM, VMEM, VMEM, VMEM, VMEM],
    )(tile, lens_weights, own_samples, other_samples, cells, first, second)[0]
    maps = lax.all_gather(local_map, "depth")
    return call(
        compose_kernel,
        [jax.ShapeDtypeStruct((6 * groups, LANES), F32)],
        [SMEM, VMEM, VMEM],
    )(depth, maps, angles)[0].reshape(1, 6, rays)


def solution(mesh):
    return jax.shard_map(
        body,
        mesh=mesh,
        in_specs=(
            P(("depth", "tile"), None, None),
            P(("depth", "tile")),
            P(("depth", "tile")),
            P("depth"),
            P("depth", "tile"),
            P(None, "tile"),
        ),
        out_specs=P("depth", None, "tile"),
        check_vma=False,
    )
```

```python
import functools

import jax
import jax.numpy as jnp
import ml_dtypes
import numpy as np
from jax import lax
from jax.experimental import pallas as pl
from jax.experimental.pallas import tpu as pltpu
from jax.sharding import PartitionSpec as P

F32 = jnp.float32
BF16 = jnp.bfloat16
LANES = 128
VMEM = pl.BlockSpec(memory_space=pltpu.VMEM)
SMEM = pl.BlockSpec(memory_space=pltpu.SMEM)
HBM = pl.BlockSpec(memory_space=pltpu.HBM)


def call(kernel, outs, in_specs, scratch=(), limit=48, flops=0, moved=0):
    return pl.pallas_call(
        kernel,
        out_shape=outs,
        in_specs=in_specs,
        out_specs=jax.tree.map(lambda _: VMEM, outs),
        scratch_shapes=list(scratch),
        compiler_params=pltpu.CompilerParams(vmem_limit_bytes=limit << 20),
        cost_estimate=pl.CostEstimate(flops=flops, bytes_accessed=moved, transcendentals=0),
    )


def mul(a, b):
    return jnp.dot(a, b, preferred_element_type=F32)


def halves(a):
    high = a.astype(BF16)
    return high, (a - high.astype(F32)).astype(BF16)


def label_rows(capacity):
    return -(-capacity // 16) * 16


def tables(side):
    index = np.arange(side, dtype=np.float64) + 1.0
    sines = np.sqrt(2.0 / (side + 1.0)) * np.sin(np.pi * index[:, None] * index[None, :] / (side + 1.0))
    high = sines.astype(np.float32).astype(ml_dtypes.bfloat16)
    low = (sines - high.astype(np.float64)).astype(np.float32).astype(ml_dtypes.bfloat16)
    single = 2.0 - 2.0 * np.cos(np.pi * index / (side + 1.0))
    inverse = -2.0 / (single[:, None] + single[None, :])
    return high, low, inverse.astype(np.float32)


def pack_kernel(tile_count, capacity, layout, tile_ref, owner_ref, place_ref, blocks_ref, *rest):
    outs, slot_ref, count_ref = rest[-2 - len(layout) : -2], rest[-2], rest[-1]
    slots, side = blocks_ref.shape[0], blocks_ref.shape[1]
    spare = tile_count * capacity
    tile = tile_ref[0]
    for x in range(tile_count + 1):
        count_ref[x] = 0
    for i in range(spare):
        slot_ref[i] = -1
    for e in range(slots):
        owner = owner_ref[e]
        live = owner < tile_count
        chunk = jnp.where(live, owner ^ tile, tile_count)
        count = count_ref[chunk]
        count_ref[chunk] = count + 1
        slot_ref[jnp.where(live, chunk * capacity + count, spare + e)] = e
    rows = label_rows(capacity)
    row = lax.broadcasted_iota(jnp.int32, (rows, side), 0)
    for out, members in zip(outs, layout):
        for i, x in enumerate(members):
            base = i * (capacity * side + rows)
            labels = jnp.full((rows, side), -1, jnp.int32)
            for c in range(capacity):
                entry = slot_ref[x * capacity + c]
                safe = jnp.maximum(entry, 0)
                label = jnp.where(entry >= 0, place_ref[safe], -1)
                out[pl.ds(base + c * side, side), :] = blocks_ref[safe]
                labels = jnp.where(row == c, label, labels)
            out[pl.ds(base + capacity * side, rows), :] = labels.astype(F32).astype(BF16)


def solve_kernel(capacity, planes, *refs):
    high_ref, low_ref, inverse_ref = refs[:3]
    chunks, (p_ref, c_ref, edge_ref) = refs[3:-3], refs[-3:]
    side = chunks[0].shape[1]
    for k in range(planes):
        c_ref[k] = jnp.zeros(c_ref.shape[1:], BF16)
    rows = label_rows(capacity)
    for chunk in chunks:
        labels = chunk[pl.ds(capacity * side, rows), :].astype(F32).astype(jnp.int32)
        for c in range(capacity):
            label = labels[c, 0]
            plane = jnp.where(label >= 0, label >> 2, planes)
            top = pl.multiple_of(((label >> 1) & 1) * side, side)
            left = pl.multiple_of((label & 1) * side, side)
            c_ref[plane, pl.ds(top, side), pl.ds(left, side)] = chunk[pl.ds(c * side, side), :]

    high, low, inverse = high_ref[...], low_ref[...], inverse_ref[...]
    across = jnp.concatenate([high, high, low], axis=1)
    down = jnp.concatenate([high, high, low], axis=0)
    pair = jnp.concatenate([high, low], axis=0)

    def right(a, b):
        return mul(jnp.concatenate([a, b, a], axis=1), down)

    def left(a, b):
        return mul(across, jnp.concatenate([a, b, a], axis=0))

    mass = [c_ref[k] for k in range(planes)]
    parts = [halves(mul(jnp.concatenate([m, m], axis=1), pair)) for m in mass]
    parts = [halves(left(*part) * inverse) for part in parts]
    parts = [halves(right(*part)) for part in parts]
    for k in range(planes):
        potential = left(*parts[k])
        p_ref[k] = potential
        for i in range(2 * side // LANES):
            part = potential[:, i * LANES : (i + 1) * LANES]
            edge_ref[pl.ds(2 * i * planes + k, 1), :] = part[:1]
            edge_ref[pl.ds((2 * i + 1) * planes + k, 1), :] = part[2 * side - 1 :]


def shifted(a, axis, step):
    size = a.shape[axis]
    tile = 8 if axis == 0 and size > 8 else min(size, LANES)
    rolled = pltpu.roll(a, (-step) % size, axis)
    at = size - tile if step > 0 else 0
    last = lax.slice_in_dim(rolled, at, at + tile, axis=axis)
    place = lax.broadcasted_iota(jnp.int32, last.shape, axis)
    last = jnp.where(place == (tile - 1 if step > 0 else 0), 0.0, last)
    if size == tile:
        return last
    if step > 0:
        return jnp.concatenate([lax.slice_in_dim(rolled, 0, at, axis=axis), last], axis=axis)
    return jnp.concatenate([last, lax.slice_in_dim(rolled, tile, size, axis=axis)], axis=axis)


def pick_kernel(planes, used, p_ref, c_ref, cells_ref, *refs):
    last_ref, out_ref = refs[-2:]
    start = used[0]
    if len(refs) > 2:
        rest = refs[0][...]
        count = rest.shape[0]
        for i in range(3):
            part = rest.astype(BF16)
            last_ref[pl.ds(out_ref.shape[0] + i * count, count), :] = part
            rest = rest - part.astype(F32)
    side = p_ref.shape[1]
    shift = side.bit_length() - 1
    groups = cells_ref.shape[0] // planes
    width = 2 if groups % 2 == 0 else 1
    sub = lax.broadcasted_iota(jnp.int32, (8, width * LANES), 0)
    column = lax.broadcasted_iota(jnp.int32, (side, width * LANES), 0)
    for k in used:
        p = p_ref[k]
        above, below = shifted(p, 0, -1), shifted(p, 0, 1)
        left, right = shifted(p, 1, -1), shifted(p, 1, 1)
        tilt = 0.5 * (right - left)
        fields = (
            (0.5 * (below - above)).astype(BF16),
            tilt.astype(BF16),
            c_ref[k],
            (0.5 * ((below + above) - (right + left))).astype(BF16),
            (0.5 * (shifted(tilt, 0, 1) - shifted(tilt, 0, -1))).astype(BF16),
        )
        for g in range(0, groups, width):
            cells = jnp.concatenate([cells_ref[pl.ds(k * groups + g + w, 1), :] for w in range(width)], axis=1)
            row, col = cells >> shift, cells & (side - 1)
            chosen = (column == col).astype(F32).astype(BF16)
            block, within = row >> 3, sub == (row & 7)
            bits = [(block >> i) & 1 == 1 for i in range((side // 8).bit_length() - 1)]
            for f in range(5):
                picked = mul(fields[f], chosen)
                kept = [picked[v * 8 : v * 8 + 8] for v in range(side // 8)]
                for bit in bits:
                    kept = [jnp.where(bit, b, a) for a, b in zip(kept[::2], kept[1::2])]
                value = jnp.sum(jnp.where(within, kept[0], 0.0), axis=0, keepdims=True)
                for w in range(width):
                    out_ref[pl.ds(((k - start) * 5 + f) * groups + g + w, 1), :] = value[:, w * LANES : (w + 1) * LANES]
    last_ref[pl.ds(0, out_ref.shape[0]), :] = out_ref[...].astype(last_ref.dtype)


def taken(table, index):
    parts = table.shape[1] // LANES
    rows = index.shape[0]
    lane, part = index & (LANES - 1), index >> 7
    out = None
    for i in range(parts):
        spread = jnp.broadcast_to(table[:, i * LANES : (i + 1) * LANES], (rows, LANES))
        got = jnp.take_along_axis(spread, lane, axis=1, mode="promise_in_bounds")
        out = got if out is None else jnp.where(part == i, got, out)
    return out


def edge_kernel(planes, tile_ref, ours_ref, crossed_ref, first_ref, second_ref):
    count = ours_ref.shape[0]
    even = (tile_ref[0] & 1) == 0
    total = ours_ref[...]
    begin = crossed_ref.shape[0] - 3 * count
    for i in range(3):
        total = total + crossed_ref[pl.ds(begin + i * count, count), :].astype(F32)
    for i in range(count // (2 * planes)):
        top = total[2 * i * planes : (2 * i + 1) * planes]
        end = total[(2 * i + 1) * planes : (2 * i + 2) * planes]
        first_ref[pl.ds(i * planes, planes), :] = jnp.where(even, end, top)
        second_ref[pl.ds(i * planes, planes), :] = jnp.where(even, top, end)


def combine_kernel(tile_count, planes, side, tile_ref, weights_ref, cells_ref, first_ref, second_ref, early_ref, late_ref, two_ref, out_ref):
    groups = cells_ref.shape[0] // planes
    shift = side.bit_length() - 1
    tile = tile_ref[0]
    even = (tile & 1) == 0
    starts, ends = tile == 0, tile == tile_count - 1
    axx = ayy = jnp.ones((groups, LANES), F32)
    axy = ayx = bx = by = jnp.zeros((groups, LANES), F32)
    for k in range(planes):
        cells = cells_ref[pl.ds(k * groups, groups), :]
        row, col = cells >> shift, cells & (side - 1)
        first, second = (
            jnp.concatenate([ref[pl.ds(i * planes + k, 1), :] for i in range(side // LANES)], axis=1)
            for ref in (first_ref, second_ref)
        )
        above, below = jnp.where(even, second, first), jnp.where(even, first, second)
        above, below = jnp.where(starts, 0.0, above), jnp.where(ends, 0.0, below)
        at_top, at_end = row == 0, row == side - 1
        up, down = taken(above, col), taken(below, col)
        up_x = taken(shifted(above, 1, 1) - shifted(above, 1, -1), col)
        down_x = taken(shifted(below, 1, 1) - shifted(below, 1, -1), col)
        near = jnp.where(at_top, up, 0.0)
        far = jnp.where(at_end, down, 0.0)
        cross = 0.25 * (jnp.where(at_end, down_x, 0.0) - jnp.where(at_top, up_x, 0.0))

        def read(f):
            early = early_ref.shape[0] // (5 * groups)
            one_ref, j = (early_ref, k) if k < early else (late_ref, k - early)
            other = two_ref[pl.ds((k * 5 + f) * groups, groups), :]
            return one_ref[pl.ds((j * 5 + f) * groups, groups), :] + other.astype(F32)

        weight = weights_ref[k]
        bend_x, bend_y = read(0) + 0.5 * (far - near), read(1)
        extra = 0.5 * (far + near)
        kappa, shear, mixed = read(2) + extra, read(3) + extra, read(4) + cross
        upper, lower = weight * (kappa + shear), weight * (kappa - shear)
        mixed = weight * mixed
        axx, ayx = axx - (upper * axx + mixed * ayx), ayx - (mixed * axx + lower * ayx)
        axy, ayy = axy - (upper * axy + mixed * ayy), ayy - (mixed * axy + lower * ayy)
        bx, by = bx - weight * bend_x, by - weight * bend_y
    for i, value in enumerate((axx, axy, ayx, ayy, bx, by)):
        out_ref[pl.ds(i * groups, groups), :] = value


def compose_kernel(depth_ref, maps_ref, angles_ref, out_ref):
    count = maps_ref.shape[0]
    groups = maps_ref.shape[1] // 6
    depth = depth_ref[0]

    def part(d, i):
        return maps_ref[d, pl.ds(i * groups, groups), :]

    xx, xy, yx, yy, bx, by = (part(0, i) for i in range(6))
    for d in range(1, count):
        used = d <= depth
        mxx, mxy, myx, myy, mbx, mby = (part(d, i) for i in range(6))
        nxx, nxy = mxx * xx + mxy * yx, mxx * xy + mxy * yy
        nyx, nyy = myx * xx + myy * yx, myx * xy + myy * yy
        new = (nxx, nxy, nyx, nyy, bx + mbx, by + mby)
        xx, xy, yx, yy, bx, by = (jnp.where(used, a, b) for a, b in zip(new, (xx, xy, yx, yy, bx, by)))
    bx = bx + angles_ref[pl.ds(0, groups), :]
    by = by + angles_ref[pl.ds(groups, groups), :]
    for i, value in enumerate((xx, xy, yx, yy, bx, by)):
        out_ref[pl.ds(i * groups, groups), :] = value


def body(density_blocks, block_owner, block_place, lens_weights, ray_cells, ray_angles):
    slots, block_side = density_blocks.shape[:2]
    side = 2 * block_side
    planes, rays = ray_cells.shape
    groups = rays // LANES
    tile_count = lax.axis_size("tile")
    capacity = slots // tile_count
    half = tile_count // 2
    tile = lax.axis_index("tile").astype(jnp.int32).reshape(1)
    depth = lax.axis_index("depth").astype(jnp.int32).reshape(1)
    high, low, inverse = (jnp.asarray(t) for t in tables(side))
    cells = ray_cells.reshape(planes * groups, LANES)
    angles = ray_angles.reshape(2 * groups, LANES)

    def swap(array, bits):
        return lax.ppermute(array, "tile", [(i, i ^ bits) for i in range(tile_count)])

    rows = capacity * block_side + label_rows(capacity)
    order = list(range(2, half)) + [1]
    layout = [[half + x] for x in order] + [[half]] + [[x] for x in order] + [[0]]
    packed = call(
        functools.partial(pack_kernel, tile_count, capacity, layout),
        [jax.ShapeDtypeStruct((rows, block_side), BF16)] * tile_count,
        [SMEM, SMEM, SMEM, VMEM],
        [pltpu.SMEM((tile_count * capacity + slots,), jnp.int32), pltpu.SMEM((tile_count + 1,), jnp.int32)],
        moved=2 * density_blocks.size,
    )(tile, block_owner, block_place, density_blocks)
    theirs = [swap(chunk, x) for x, chunk in zip(order, packed)] + [packed[half - 1]]
    ours = [swap(chunk, x) for x, chunk in zip(order, packed[half:])] + [packed[-1]]
    their_cells = swap(cells, half)

    def solve(arrays):
        return call(
            functools.partial(solve_kernel, capacity, planes),
            [
                jax.ShapeDtypeStruct((planes, side, side), F32),
                jax.ShapeDtypeStruct((planes + 1, side, side), BF16),
                jax.ShapeDtypeStruct((2 * planes * side // LANES, LANES), F32),
            ],
            [VMEM] * (3 + len(arrays)),
        )(high, low, inverse, *arrays)

    def pick(used, potential, mass, at, dtype, *edges):
        count = len(used) * 5 * groups
        return call(
            functools.partial(pick_kernel, planes, used),
            [jax.ShapeDtypeStruct((count + sum(3 * e.shape[0] for e in edges), LANES), dtype)],
            [VMEM] * (3 + len(edges)),
            [pltpu.VMEM((count, LANES), F32)],
            flops=2 * 5 * len(used) * side * side * rays,
        )(potential, mass, at, *edges)[0]

    potential, mass, edges = solve(theirs)
    crossed = swap(pick(range(planes), potential, mass, their_cells, BF16, edges), half)
    potential, mass, edges = solve(ours)
    cut = planes - planes // 2
    early = pick(range(cut), potential, mass, cells, F32)
    crossed, early = lax.optimization_barrier((crossed, early))
    line = jax.ShapeDtypeStruct((planes * side // LANES, LANES), F32)
    first, second = call(functools.partial(edge_kernel, planes), [line, line], [SMEM, VMEM, VMEM])(tile, edges, crossed)
    first = swap(first, 1)
    pairs = [(i, (i + 1) % tile_count) for i in range(1, tile_count, 2)]
    second = lax.ppermute(second, "tile", pairs + [(j, i) for i, j in pairs])
    late = pick(range(cut, planes), potential, mass, cells, F32)
    local_map = call(
        functools.partial(combine_kernel, tile_count, planes, side),
        [jax.ShapeDtypeStruct((6 * groups, LANES), F32)],
        [SMEM, SMEM, VMEM, VMEM, VMEM, VMEM, VMEM, VMEM],
    )(tile, lens_weights, cells, first, second, early, late, crossed)[0]
    maps = lax.all_gather(local_map, "depth")
    return call(
        compose_kernel,
        [jax.ShapeDtypeStruct((6 * groups, LANES), F32)],
        [SMEM, VMEM, VMEM],
    )(depth, maps, angles)[0].reshape(1, 6, rays)


def solution(mesh):
    return jax.shard_map(
        body,
        mesh=mesh,
        in_specs=(
            P(("depth", "tile"), None, None),
            P(("depth", "tile")),
            P(("depth", "tile")),
            P("depth"),
            P("depth", "tile"),
            P(None, "tile"),
        ),
        out_specs=P("depth", None, "tile"),
        check_vma=False,
    )
```

```python
import functools

import jax
import jax.numpy as jnp
import ml_dtypes
import numpy as np
from jax import lax
from jax.experimental import pallas as pl
from jax.experimental.pallas import tpu as pltpu
from jax.sharding import PartitionSpec as P

F32 = jnp.float32
BF16 = jnp.bfloat16
LANES = 128
VMEM = pl.BlockSpec(memory_space=pltpu.VMEM)
SMEM = pl.BlockSpec(memory_space=pltpu.SMEM)
HBM = pl.BlockSpec(memory_space=pltpu.HBM)


def call(kernel, outs, in_specs, scratch=(), limit=48, flops=0, moved=0):
    return pl.pallas_call(
        kernel,
        out_shape=outs,
        in_specs=in_specs,
        out_specs=jax.tree.map(lambda _: VMEM, outs),
        scratch_shapes=list(scratch),
        compiler_params=pltpu.CompilerParams(vmem_limit_bytes=limit << 20),
        cost_estimate=pl.CostEstimate(flops=flops, bytes_accessed=moved, transcendentals=0),
    )


def mul(a, b):
    return jnp.dot(a, b, preferred_element_type=F32)


def halves(a):
    high = a.astype(BF16)
    return high, (a - high.astype(F32)).astype(BF16)


def label_rows(capacity):
    return -(-capacity // 16) * 16


def tables(side):
    index = np.arange(side, dtype=np.float64) + 1.0
    sines = np.sqrt(2.0 / (side + 1.0)) * np.sin(np.pi * index[:, None] * index[None, :] / (side + 1.0))
    high = sines.astype(np.float32).astype(ml_dtypes.bfloat16)
    low = (sines - high.astype(np.float64)).astype(np.float32).astype(ml_dtypes.bfloat16)
    single = 2.0 - 2.0 * np.cos(np.pi * index / (side + 1.0))
    inverse = -2.0 / (single[:, None] + single[None, :])
    return high, low, inverse.astype(np.float32)


def pack_kernel(tile_count, capacity, layout, tile_ref, owner_ref, place_ref, blocks_ref, *rest):
    outs, slot_ref, count_ref = rest[-2 - len(layout) : -2], rest[-2], rest[-1]
    slots, side = blocks_ref.shape[0], blocks_ref.shape[1]
    spare = tile_count * capacity
    tile = tile_ref[0]
    for x in range(tile_count + 1):
        count_ref[x] = 0
    for i in range(spare):
        slot_ref[i] = -1
    for e in range(slots):
        owner = owner_ref[e]
        live = owner < tile_count
        chunk = jnp.where(live, owner ^ tile, tile_count)
        count = count_ref[chunk]
        count_ref[chunk] = count + 1
        slot_ref[jnp.where(live, chunk * capacity + count, spare + e)] = e
    rows = label_rows(capacity)
    row = lax.broadcasted_iota(jnp.int32, (rows, side), 0)
    for out, members in zip(outs, layout):
        for i, x in enumerate(members):
            base = i * (capacity * side + rows)
            labels = jnp.full((rows, side), -1, jnp.int32)
            for c in range(capacity):
                entry = slot_ref[x * capacity + c]
                safe = jnp.maximum(entry, 0)
                label = jnp.where(entry >= 0, place_ref[safe], -1)
                out[pl.ds(base + c * side, side), :] = blocks_ref[safe]
                labels = jnp.where(row == c, label, labels)
            out[pl.ds(base + capacity * side, rows), :] = labels.astype(F32).astype(BF16)


def solve_kernel(capacity, planes, *refs):
    high_ref, low_ref, inverse_ref = refs[:3]
    chunks, (p_ref, c_ref, edge_ref) = refs[3:-3], refs[-3:]
    side = chunks[0].shape[1]
    for k in range(planes):
        c_ref[k] = jnp.zeros(c_ref.shape[1:], BF16)
    rows = label_rows(capacity)
    for chunk in chunks:
        labels = chunk[pl.ds(capacity * side, rows), :].astype(F32).astype(jnp.int32)
        for c in range(capacity):
            label = labels[c, 0]
            plane = jnp.where(label >= 0, label >> 2, planes)
            top = pl.multiple_of(((label >> 1) & 1) * side, side)
            left = pl.multiple_of((label & 1) * side, side)
            c_ref[plane, pl.ds(top, side), pl.ds(left, side)] = chunk[pl.ds(c * side, side), :]

    high, low, inverse = high_ref[...], low_ref[...], inverse_ref[...]
    across = jnp.concatenate([high, high, low], axis=1)
    down = jnp.concatenate([high, high, low], axis=0)
    pair = jnp.concatenate([high, low], axis=0)

    def right(a, b):
        return mul(jnp.concatenate([a, b, a], axis=1), down)

    def left(a, b):
        return mul(across, jnp.concatenate([a, b, a], axis=0))

    mass = [c_ref[k] for k in range(planes)]
    parts = [halves(mul(jnp.concatenate([m, m], axis=1), pair)) for m in mass]
    parts = [halves(left(*part) * inverse) for part in parts]
    parts = [halves(right(*part)) for part in parts]
    for k in range(planes):
        potential = left(*parts[k])
        p_ref[k] = potential
        for i in range(2 * side // LANES):
            part = potential[:, i * LANES : (i + 1) * LANES]
            edge_ref[pl.ds(2 * i * planes + k, 1), :] = part[:1]
            edge_ref[pl.ds((2 * i + 1) * planes + k, 1), :] = part[2 * side - 1 :]


def shifted(a, axis, step):
    size = a.shape[axis]
    tile = 8 if axis == 0 and size > 8 else min(size, LANES)
    rolled = pltpu.roll(a, (-step) % size, axis)
    at = size - tile if step > 0 else 0
    last = lax.slice_in_dim(rolled, at, at + tile, axis=axis)
    place = lax.broadcasted_iota(jnp.int32, last.shape, axis)
    last = jnp.where(place == (tile - 1 if step > 0 else 0), 0.0, last)
    if size == tile:
        return last
    if step > 0:
        return jnp.concatenate([lax.slice_in_dim(rolled, 0, at, axis=axis), last], axis=axis)
    return jnp.concatenate([last, lax.slice_in_dim(rolled, tile, size, axis=axis)], axis=axis)


def pick_kernel(planes, used, p_ref, c_ref, cells_ref, *refs):
    last_ref, out_ref = refs[-2:]
    start = used[0]
    if len(refs) > 2:
        rest = refs[0][...]
        count = rest.shape[0]
        for i in range(3):
            part = rest.astype(BF16)
            last_ref[pl.ds(out_ref.shape[0] + i * count, count), :] = part
            rest = rest - part.astype(F32)
    side = p_ref.shape[1]
    shift = side.bit_length() - 1
    groups = cells_ref.shape[0] // planes
    width = 2 if groups % 2 == 0 else 1
    sub = lax.broadcasted_iota(jnp.int32, (8, width * LANES), 0)
    column = lax.broadcasted_iota(jnp.int32, (side, width * LANES), 0)
    for k in used:
        p = p_ref[k]
        above, below = shifted(p, 0, -1), shifted(p, 0, 1)
        left, right = shifted(p, 1, -1), shifted(p, 1, 1)
        tilt = 0.5 * (right - left)
        fields = (
            (0.5 * (below - above)).astype(BF16),
            tilt.astype(BF16),
            c_ref[k],
            (0.5 * ((below + above) - (right + left))).astype(BF16),
            (0.5 * (shifted(tilt, 0, 1) - shifted(tilt, 0, -1))).astype(BF16),
        )
        for g in range(0, groups, width):
            cells = jnp.concatenate([cells_ref[pl.ds(k * groups + g + w, 1), :] for w in range(width)], axis=1)
            row, col = cells >> shift, cells & (side - 1)
            chosen = (column == col).astype(F32).astype(BF16)
            block, within = row >> 3, sub == (row & 7)
            bits = [(block >> i) & 1 == 1 for i in range((side // 8).bit_length() - 1)]
            for f in range(5):
                picked = mul(fields[f], chosen)
                kept = [picked[v * 8 : v * 8 + 8] for v in range(side // 8)]
                for bit in bits:
                    kept = [jnp.where(bit, b, a) for a, b in zip(kept[::2], kept[1::2])]
                value = jnp.sum(jnp.where(within, kept[0], 0.0), axis=0, keepdims=True)
                for w in range(width):
                    out_ref[pl.ds(((k - start) * 5 + f) * groups + g + w, 1), :] = value[:, w * LANES : (w + 1) * LANES]
    last_ref[pl.ds(0, out_ref.shape[0]), :] = out_ref[...].astype(last_ref.dtype)


def taken(table, index):
    parts = table.shape[1] // LANES
    rows = index.shape[0]
    lane, part = index & (LANES - 1), index >> 7
    out = None
    for i in range(parts):
        spread = jnp.broadcast_to(table[:, i * LANES : (i + 1) * LANES], (rows, LANES))
        got = jnp.take_along_axis(spread, lane, axis=1, mode="promise_in_bounds")
        out = got if out is None else jnp.where(part == i, got, out)
    return out


def edge_kernel(planes, tile_ref, ours_ref, crossed_ref, first_ref, second_ref):
    count = ours_ref.shape[0]
    even = (tile_ref[0] & 1) == 0
    total = ours_ref[...]
    begin = crossed_ref.shape[0] - 3 * count
    for i in range(3):
        total = total + crossed_ref[pl.ds(begin + i * count, count), :].astype(F32)
    for i in range(count // (2 * planes)):
        top = total[2 * i * planes : (2 * i + 1) * planes]
        end = total[(2 * i + 1) * planes : (2 * i + 2) * planes]
        first_ref[pl.ds(i * planes, planes), :] = jnp.where(even, end, top)
        second_ref[pl.ds(i * planes, planes), :] = jnp.where(even, top, end)


def combine_kernel(tile_count, planes, side, tile_ref, weights_ref, cells_ref, first_ref, second_ref, early_ref, late_ref, two_ref, out_ref):
    groups = cells_ref.shape[0] // planes
    shift = side.bit_length() - 1
    tile = tile_ref[0]
    even = (tile & 1) == 0
    starts, ends = tile == 0, tile == tile_count - 1
    axx = ayy = jnp.ones((groups, LANES), F32)
    axy = ayx = bx = by = jnp.zeros((groups, LANES), F32)
    for k in range(planes):
        cells = cells_ref[pl.ds(k * groups, groups), :]
        row, col = cells >> shift, cells & (side - 1)
        first, second = (
            jnp.concatenate([ref[pl.ds(i * planes + k, 1), :] for i in range(side // LANES)], axis=1)
            for ref in (first_ref, second_ref)
        )
        above, below = jnp.where(even, second, first), jnp.where(even, first, second)
        above, below = jnp.where(starts, 0.0, above), jnp.where(ends, 0.0, below)
        at_top, at_end = row == 0, row == side - 1
        up, down = taken(above, col), taken(below, col)
        up_x = taken(shifted(above, 1, 1) - shifted(above, 1, -1), col)
        down_x = taken(shifted(below, 1, 1) - shifted(below, 1, -1), col)
        near = jnp.where(at_top, up, 0.0)
        far = jnp.where(at_end, down, 0.0)
        cross = 0.25 * (jnp.where(at_end, down_x, 0.0) - jnp.where(at_top, up_x, 0.0))

        def read(f):
            early = early_ref.shape[0] // (5 * groups)
            one_ref, j = (early_ref, k) if k < early else (late_ref, k - early)
            other = two_ref[pl.ds((k * 5 + f) * groups, groups), :]
            return one_ref[pl.ds((j * 5 + f) * groups, groups), :] + other.astype(F32)

        weight = weights_ref[k]
        bend_x, bend_y = read(0) + 0.5 * (far - near), read(1)
        extra = 0.5 * (far + near)
        kappa, shear, mixed = read(2) + extra, read(3) + extra, read(4) + cross
        upper, lower = weight * (kappa + shear), weight * (kappa - shear)
        mixed = weight * mixed
        axx, ayx = axx - (upper * axx + mixed * ayx), ayx - (mixed * axx + lower * ayx)
        axy, ayy = axy - (upper * axy + mixed * ayy), ayy - (mixed * axy + lower * ayy)
        bx, by = bx - weight * bend_x, by - weight * bend_y
    for i, value in enumerate((axx, axy, ayx, ayy, bx, by)):
        out_ref[pl.ds(i * groups, groups), :] = value


def compose_kernel(count, depth_ref, *refs):
    angles_ref, out_ref, maps_ref = refs[count:]
    groups = maps_ref.shape[1] // 6
    depth = depth_ref[0]
    for i in range(count):
        maps_ref[depth ^ i] = refs[i][...]

    def part(d, i):
        return maps_ref[d, pl.ds(i * groups, groups), :]

    xx, xy, yx, yy, bx, by = (part(0, i) for i in range(6))
    for d in range(1, count):
        used = d <= depth
        mxx, mxy, myx, myy, mbx, mby = (part(d, i) for i in range(6))
        nxx, nxy = mxx * xx + mxy * yx, mxx * xy + mxy * yy
        nyx, nyy = myx * xx + myy * yx, myx * xy + myy * yy
        new = (nxx, nxy, nyx, nyy, bx + mbx, by + mby)
        xx, xy, yx, yy, bx, by = (jnp.where(used, a, b) for a, b in zip(new, (xx, xy, yx, yy, bx, by)))
    bx = bx + angles_ref[pl.ds(0, groups), :]
    by = by + angles_ref[pl.ds(groups, groups), :]
    for i, value in enumerate((xx, xy, yx, yy, bx, by)):
        out_ref[pl.ds(i * groups, groups), :] = value


def body(density_blocks, block_owner, block_place, lens_weights, ray_cells, ray_angles):
    slots, block_side = density_blocks.shape[:2]
    side = 2 * block_side
    planes, rays = ray_cells.shape
    groups = rays // LANES
    tile_count = lax.axis_size("tile")
    capacity = slots // tile_count
    half = tile_count // 2
    tile = lax.axis_index("tile").astype(jnp.int32).reshape(1)
    depth = lax.axis_index("depth").astype(jnp.int32).reshape(1)
    high, low, inverse = (jnp.asarray(t) for t in tables(side))
    cells = ray_cells.reshape(planes * groups, LANES)
    angles = ray_angles.reshape(2 * groups, LANES)

    def swap(array, bits):
        return lax.ppermute(array, "tile", [(i, i ^ bits) for i in range(tile_count)])

    rows = capacity * block_side + label_rows(capacity)
    order = list(range(2, half)) + [1]
    layout = [[half + x] for x in order] + [[half]] + [[x] for x in order] + [[0]]
    packed = call(
        functools.partial(pack_kernel, tile_count, capacity, layout),
        [jax.ShapeDtypeStruct((rows, block_side), BF16)] * tile_count,
        [SMEM, SMEM, SMEM, VMEM],
        [pltpu.SMEM((tile_count * capacity + slots,), jnp.int32), pltpu.SMEM((tile_count + 1,), jnp.int32)],
        moved=2 * density_blocks.size,
    )(tile, block_owner, block_place, density_blocks)
    theirs = [swap(chunk, x) for x, chunk in zip(order, packed)] + [packed[half - 1]]
    ours = [swap(chunk, x) for x, chunk in zip(order, packed[half:])] + [packed[-1]]
    their_cells = swap(cells, half)

    def solve(arrays):
        return call(
            functools.partial(solve_kernel, capacity, planes),
            [
                jax.ShapeDtypeStruct((planes, side, side), F32),
                jax.ShapeDtypeStruct((planes + 1, side, side), BF16),
                jax.ShapeDtypeStruct((2 * planes * side // LANES, LANES), F32),
            ],
            [VMEM] * (3 + len(arrays)),
        )(high, low, inverse, *arrays)

    def pick(used, potential, mass, at, dtype, *edges):
        count = len(used) * 5 * groups
        return call(
            functools.partial(pick_kernel, planes, used),
            [jax.ShapeDtypeStruct((count + sum(3 * e.shape[0] for e in edges), LANES), dtype)],
            [VMEM] * (3 + len(edges)),
            [pltpu.VMEM((count, LANES), F32)],
            flops=2 * 5 * len(used) * side * side * rays,
        )(potential, mass, at, *edges)[0]

    potential, mass, edges = solve(theirs)
    crossed = swap(pick(range(planes), potential, mass, their_cells, BF16, edges), half)
    potential, mass, edges = solve(ours)
    cut = planes - planes // 2
    early = pick(range(cut), potential, mass, cells, F32)
    crossed, early = lax.optimization_barrier((crossed, early))
    line = jax.ShapeDtypeStruct((planes * side // LANES, LANES), F32)
    first, second = call(functools.partial(edge_kernel, planes), [line, line], [SMEM, VMEM, VMEM])(tile, edges, crossed)
    first = swap(first, 1)
    pairs = [(i, (i + 1) % tile_count) for i in range(1, tile_count, 2)]
    second = lax.ppermute(second, "tile", pairs + [(j, i) for i, j in pairs])
    late = pick(range(cut, planes), potential, mass, cells, F32)
    local_map = call(
        functools.partial(combine_kernel, tile_count, planes, side),
        [jax.ShapeDtypeStruct((6 * groups, LANES), F32)],
        [SMEM, SMEM, VMEM, VMEM, VMEM, VMEM, VMEM, VMEM],
    )(tile, lens_weights, cells, first, second, early, late, crossed)[0]
    count = lax.axis_size("depth")
    maps = [local_map]
    maps += [lax.ppermute(local_map, "depth", [(i, i ^ d) for i in range(count)]) for d in range(1, count)]
    return call(
        functools.partial(compose_kernel, count),
        [jax.ShapeDtypeStruct((6 * groups, LANES), F32)],
        [SMEM] + [VMEM] * (count + 1),
        [pltpu.VMEM((count, 6 * groups, LANES), F32)],
    )(depth, *maps, angles)[0].reshape(1, 6, rays)


def solution(mesh):
    return jax.shard_map(
        body,
        mesh=mesh,
        in_specs=(
            P(("depth", "tile"), None, None),
            P(("depth", "tile")),
            P(("depth", "tile")),
            P("depth"),
            P("depth", "tile"),
            P(None, "tile"),
        ),
        out_specs=P("depth", None, "tile"),
        check_vma=False,
    )
```

```python
import functools

import jax
import jax.numpy as jnp
import ml_dtypes
import numpy as np
from jax import lax
from jax.experimental import pallas as pl
from jax.experimental.pallas import tpu as pltpu
from jax.sharding import PartitionSpec as P

F32 = jnp.float32
BF16 = jnp.bfloat16
LANES = 128
VMEM = pl.BlockSpec(memory_space=pltpu.VMEM)
SMEM = pl.BlockSpec(memory_space=pltpu.SMEM)
HBM = pl.BlockSpec(memory_space=pltpu.HBM)


def call(kernel, outs, in_specs, scratch=(), limit=48, flops=0, moved=0):
    return pl.pallas_call(
        kernel,
        out_shape=outs,
        in_specs=in_specs,
        out_specs=jax.tree.map(lambda _: VMEM, outs),
        scratch_shapes=list(scratch),
        compiler_params=pltpu.CompilerParams(vmem_limit_bytes=limit << 20),
        cost_estimate=pl.CostEstimate(flops=flops, bytes_accessed=moved, transcendentals=0),
    )


def mul(a, b):
    return jnp.dot(a, b, preferred_element_type=F32)


def halves(a):
    high = a.astype(BF16)
    return high, (a - high.astype(F32)).astype(BF16)


def label_rows(capacity):
    return -(-capacity // 16) * 16


def tables(side):
    index = np.arange(side, dtype=np.float64) + 1.0
    sines = np.sqrt(2.0 / (side + 1.0)) * np.sin(np.pi * index[:, None] * index[None, :] / (side + 1.0))
    high = sines.astype(np.float32).astype(ml_dtypes.bfloat16)
    low = (sines - high.astype(np.float64)).astype(np.float32).astype(ml_dtypes.bfloat16)
    single = 2.0 - 2.0 * np.cos(np.pi * index / (side + 1.0))
    inverse = -2.0 / (single[:, None] + single[None, :])
    return high, low, inverse.astype(np.float32)


def pack_kernel(tile_count, capacity, layout, tile_ref, owner_ref, place_ref, blocks_ref, *rest):
    outs, slot_ref, count_ref = rest[-2 - len(layout) : -2], rest[-2], rest[-1]
    slots, side = blocks_ref.shape[0], blocks_ref.shape[1]
    spare = tile_count * capacity
    tile = tile_ref[0]
    for x in range(tile_count + 1):
        count_ref[x] = 0
    for i in range(spare):
        slot_ref[i] = -1
    for e in range(slots):
        owner = owner_ref[e]
        live = owner < tile_count
        chunk = jnp.where(live, owner ^ tile, tile_count)
        count = count_ref[chunk]
        count_ref[chunk] = count + 1
        slot_ref[jnp.where(live, chunk * capacity + count, spare + e)] = e
    rows = label_rows(capacity)
    row = lax.broadcasted_iota(jnp.int32, (rows, side), 0)
    for out, members in zip(outs, layout):
        for i, x in enumerate(members):
            base = i * (capacity * side + rows)
            labels = jnp.full((rows, side), -1, jnp.int32)
            for c in range(capacity):
                entry = slot_ref[x * capacity + c]
                safe = jnp.maximum(entry, 0)
                label = jnp.where(entry >= 0, place_ref[safe], -1)
                out[pl.ds(base + c * side, side), :] = blocks_ref[safe]
                labels = jnp.where(row == c, label, labels)
            out[pl.ds(base + capacity * side, rows), :] = labels.astype(F32).astype(BF16)


def solve_kernel(capacity, planes, *refs):
    high_ref, low_ref, inverse_ref = refs[:3]
    chunks, (p_ref, c_ref, edge_ref) = refs[3:-3], refs[-3:]
    side = chunks[0].shape[1]
    for k in range(planes):
        c_ref[k] = jnp.zeros(c_ref.shape[1:], BF16)
    rows = label_rows(capacity)
    for chunk in chunks:
        labels = chunk[pl.ds(capacity * side, rows), :].astype(F32).astype(jnp.int32)
        for c in range(capacity):
            label = labels[c, 0]
            plane = jnp.where(label >= 0, label >> 2, planes)
            top = pl.multiple_of(((label >> 1) & 1) * side, side)
            left = pl.multiple_of((label & 1) * side, side)
            c_ref[plane, pl.ds(top, side), pl.ds(left, side)] = chunk[pl.ds(c * side, side), :]

    high, low, inverse = high_ref[...], low_ref[...], inverse_ref[...]
    across = jnp.concatenate([high, high, low], axis=1)
    down = jnp.concatenate([high, high, low], axis=0)
    pair = jnp.concatenate([high, low], axis=0)

    def right(a, b):
        return mul(jnp.concatenate([a, b, a], axis=1), down)

    def left(a, b):
        return mul(across, jnp.concatenate([a, b, a], axis=0))

    mass = [c_ref[k] for k in range(planes)]
    parts = [halves(mul(jnp.concatenate([m, m], axis=1), pair)) for m in mass]
    parts = [halves(left(*part) * inverse) for part in parts]
    parts = [halves(right(*part)) for part in parts]
    for k in range(planes):
        potential = left(*parts[k])
        p_ref[k] = potential
        for i in range(2 * side // LANES):
            part = potential[:, i * LANES : (i + 1) * LANES]
            edge_ref[pl.ds(2 * i * planes + k, 1), :] = part[:1]
            edge_ref[pl.ds((2 * i + 1) * planes + k, 1), :] = part[2 * side - 1 :]


def shifted(a, axis, step):
    size = a.shape[axis]
    tile = 8 if axis == 0 and size > 8 else min(size, LANES)
    rolled = pltpu.roll(a, (-step) % size, axis)
    at = size - tile if step > 0 else 0
    last = lax.slice_in_dim(rolled, at, at + tile, axis=axis)
    place = lax.broadcasted_iota(jnp.int32, last.shape, axis)
    last = jnp.where(place == (tile - 1 if step > 0 else 0), 0.0, last)
    if size == tile:
        return last
    if step > 0:
        return jnp.concatenate([lax.slice_in_dim(rolled, 0, at, axis=axis), last], axis=axis)
    return jnp.concatenate([last, lax.slice_in_dim(rolled, tile, size, axis=axis)], axis=axis)


def pick_kernel(planes, used, p_ref, c_ref, cells_ref, *refs):
    last_ref, out_ref = refs[-2:]
    start = used[0]
    if len(refs) > 2:
        rest = refs[0][...]
        count = rest.shape[0]
        for i in range(3):
            part = rest.astype(BF16)
            last_ref[pl.ds(out_ref.shape[0] + i * count, count), :] = part
            rest = rest - part.astype(F32)
    side = p_ref.shape[1]
    shift = side.bit_length() - 1
    groups = cells_ref.shape[0] // planes
    width = 2 if groups % 2 == 0 else 1
    sub = lax.broadcasted_iota(jnp.int32, (8, width * LANES), 0)
    column = lax.broadcasted_iota(jnp.int32, (side, width * LANES), 0)
    for k in used:
        p = p_ref[k]
        above, below = shifted(p, 0, -1), shifted(p, 0, 1)
        left, right = shifted(p, 1, -1), shifted(p, 1, 1)
        tilt = 0.5 * (right - left)
        fields = (
            (0.5 * (below - above)).astype(BF16),
            tilt.astype(BF16),
            c_ref[k],
            (0.5 * ((below + above) - (right + left))).astype(BF16),
            (0.5 * (shifted(tilt, 0, 1) - shifted(tilt, 0, -1))).astype(BF16),
        )
        for g in range(0, groups, width):
            cells = jnp.concatenate([cells_ref[pl.ds(k * groups + g + w, 1), :] for w in range(width)], axis=1)
            row, col = cells >> shift, cells & (side - 1)
            chosen = (column == col).astype(F32).astype(BF16)
            block, within = row >> 3, sub == (row & 7)
            bits = [(block >> i) & 1 == 1 for i in range((side // 8).bit_length() - 1)]
            for f in range(5):
                picked = mul(fields[f], chosen)
                kept = [picked[v * 8 : v * 8 + 8] for v in range(side // 8)]
                for bit in bits:
                    kept = [jnp.where(bit, b, a) for a, b in zip(kept[::2], kept[1::2])]
                value = jnp.sum(jnp.where(within, kept[0], 0.0), axis=0, keepdims=True)
                for w in range(width):
                    out_ref[pl.ds(((k - start) * 5 + f) * groups + g + w, 1), :] = value[:, w * LANES : (w + 1) * LANES]
    last_ref[pl.ds(0, out_ref.shape[0]), :] = out_ref[...].astype(last_ref.dtype)


def taken(table, index):
    parts = table.shape[1] // LANES
    rows = index.shape[0]
    lane, part = index & (LANES - 1), index >> 7
    out = None
    for i in range(parts):
        spread = jnp.broadcast_to(table[:, i * LANES : (i + 1) * LANES], (rows, LANES))
        got = jnp.take_along_axis(spread, lane, axis=1, mode="promise_in_bounds")
        out = got if out is None else jnp.where(part == i, got, out)
    return out


def edge_kernel(planes, tile_ref, ours_ref, crossed_ref, first_ref, second_ref):
    count = ours_ref.shape[0]
    even = (tile_ref[0] & 1) == 0
    total = ours_ref[...]
    begin = crossed_ref.shape[0] - 3 * count
    for i in range(3):
        total = total + crossed_ref[pl.ds(begin + i * count, count), :].astype(F32)
    for i in range(count // (2 * planes)):
        top = total[2 * i * planes : (2 * i + 1) * planes]
        end = total[(2 * i + 1) * planes : (2 * i + 2) * planes]
        first_ref[pl.ds(i * planes, planes), :] = jnp.where(even, end, top)
        second_ref[pl.ds(i * planes, planes), :] = jnp.where(even, top, end)


def combine_kernel(tile_count, planes, side, tile_ref, weights_ref, cells_ref, first_ref, second_ref, early_ref, late_ref, two_ref, out_ref):
    groups = cells_ref.shape[0] // planes
    shift = side.bit_length() - 1
    tile = tile_ref[0]
    even = (tile & 1) == 0
    starts, ends = tile == 0, tile == tile_count - 1
    axx = ayy = jnp.ones((groups, LANES), F32)
    axy = ayx = bx = by = jnp.zeros((groups, LANES), F32)
    for k in range(planes):
        cells = cells_ref[pl.ds(k * groups, groups), :]
        row, col = cells >> shift, cells & (side - 1)
        first, second = (
            jnp.concatenate([ref[pl.ds(i * planes + k, 1), :] for i in range(side // LANES)], axis=1)
            for ref in (first_ref, second_ref)
        )
        above, below = jnp.where(even, second, first), jnp.where(even, first, second)
        above, below = jnp.where(starts, 0.0, above), jnp.where(ends, 0.0, below)
        at_top, at_end = row == 0, row == side - 1
        up, down = taken(above, col), taken(below, col)
        up_x = taken(shifted(above, 1, 1) - shifted(above, 1, -1), col)
        down_x = taken(shifted(below, 1, 1) - shifted(below, 1, -1), col)
        near = jnp.where(at_top, up, 0.0)
        far = jnp.where(at_end, down, 0.0)
        cross = 0.25 * (jnp.where(at_end, down_x, 0.0) - jnp.where(at_top, up_x, 0.0))

        def read(f):
            early = early_ref.shape[0] // (5 * groups)
            one_ref, j = (early_ref, k) if k < early else (late_ref, k - early)
            other = two_ref[pl.ds((k * 5 + f) * groups, groups), :]
            return one_ref[pl.ds((j * 5 + f) * groups, groups), :] + other.astype(F32)

        weight = weights_ref[k]
        bend_x, bend_y = read(0) + 0.5 * (far - near), read(1)
        extra = 0.5 * (far + near)
        kappa, shear, mixed = read(2) + extra, read(3) + extra, read(4) + cross
        upper, lower = weight * (kappa + shear), weight * (kappa - shear)
        mixed = weight * mixed
        axx, ayx = axx - (upper * axx + mixed * ayx), ayx - (mixed * axx + lower * ayx)
        axy, ayy = axy - (upper * axy + mixed * ayy), ayy - (mixed * axy + lower * ayy)
        bx, by = bx - weight * bend_x, by - weight * bend_y
    for i, value in enumerate((axx, axy, ayx, ayy, bx, by)):
        out_ref[pl.ds(i * groups, groups), :] = value


def compose_kernel(count, depth_ref, *refs):
    angles_ref, out_ref, maps_ref = refs[count:]
    groups = maps_ref.shape[1] // 6
    depth = depth_ref[0]
    for i in range(count):
        maps_ref[depth ^ i] = refs[i][...]

    def part(d, i):
        return maps_ref[d, pl.ds(i * groups, groups), :]

    xx, xy, yx, yy, bx, by = (part(0, i) for i in range(6))
    for d in range(1, count):
        used = d <= depth
        mxx, mxy, myx, myy, mbx, mby = (part(d, i) for i in range(6))
        nxx, nxy = mxx * xx + mxy * yx, mxx * xy + mxy * yy
        nyx, nyy = myx * xx + myy * yx, myx * xy + myy * yy
        new = (nxx, nxy, nyx, nyy, bx + mbx, by + mby)
        xx, xy, yx, yy, bx, by = (jnp.where(used, a, b) for a, b in zip(new, (xx, xy, yx, yy, bx, by)))
    bx = bx + angles_ref[pl.ds(0, groups), :]
    by = by + angles_ref[pl.ds(groups, groups), :]
    for i, value in enumerate((xx, xy, yx, yy, bx, by)):
        out_ref[pl.ds(i * groups, groups), :] = value


def body(density_blocks, block_owner, block_place, lens_weights, ray_cells, ray_angles):
    slots, block_side = density_blocks.shape[:2]
    side = 2 * block_side
    planes, rays = ray_cells.shape
    groups = rays // LANES
    tile_count = lax.axis_size("tile")
    capacity = slots // tile_count
    half = tile_count // 2
    tile = lax.axis_index("tile").astype(jnp.int32).reshape(1)
    depth = lax.axis_index("depth").astype(jnp.int32).reshape(1)
    high, low, inverse = (jnp.asarray(t) for t in tables(side))
    cells = ray_cells.reshape(planes * groups, LANES)
    angles = ray_angles.reshape(2 * groups, LANES)

    def swap(array, bits):
        return lax.ppermute(array, "tile", [(i, i ^ bits) for i in range(tile_count)])

    rows = capacity * block_side + label_rows(capacity)
    order = list(range(2, half)) + [1]
    layout = [[half + x] for x in order] + [[half]] + [[x] for x in order] + [[0]]
    packed = call(
        functools.partial(pack_kernel, tile_count, capacity, layout),
        [jax.ShapeDtypeStruct((rows, block_side), BF16)] * tile_count,
        [SMEM, SMEM, SMEM, VMEM],
        [pltpu.SMEM((tile_count * capacity + slots,), jnp.int32), pltpu.SMEM((tile_count + 1,), jnp.int32)],
        moved=2 * density_blocks.size,
    )(tile, block_owner, block_place, density_blocks)
    theirs = [swap(chunk, x) for x, chunk in zip(order, packed)] + [packed[half - 1]]
    ours = [swap(chunk, x) for x, chunk in zip(order, packed[half:])] + [packed[-1]]
    their_cells = swap(cells, half)

    def solve(arrays):
        return call(
            functools.partial(solve_kernel, capacity, planes),
            [
                jax.ShapeDtypeStruct((planes, side, side), F32),
                jax.ShapeDtypeStruct((planes + 1, side, side), BF16),
                jax.ShapeDtypeStruct((2 * planes * side // LANES, LANES), F32),
            ],
            [VMEM] * (3 + len(arrays)),
        )(high, low, inverse, *arrays)

    def pick(used, potential, mass, at, dtype, *edges):
        count = len(used) * 5 * groups
        return call(
            functools.partial(pick_kernel, planes, used),
            [jax.ShapeDtypeStruct((count + sum(3 * e.shape[0] for e in edges), LANES), dtype)],
            [VMEM] * (3 + len(edges)),
            [pltpu.VMEM((count, LANES), F32)],
            flops=2 * 5 * len(used) * side * side * rays,
        )(potential, mass, at, *edges)[0]

    potential, mass, edges = solve(theirs)
    crossed = swap(pick(range(planes), potential, mass, their_cells, BF16, edges), half)
    potential, mass, edges = solve(ours)
    cut = planes - planes // 4
    early = pick(range(cut), potential, mass, cells, F32)
    crossed, early = lax.optimization_barrier((crossed, early))
    line = jax.ShapeDtypeStruct((planes * side // LANES, LANES), F32)
    first, second = call(functools.partial(edge_kernel, planes), [line, line], [SMEM, VMEM, VMEM])(tile, edges, crossed)
    first = swap(first, 1)
    pairs = [(i, (i + 1) % tile_count) for i in range(1, tile_count, 2)]
    second = lax.ppermute(second, "tile", pairs + [(j, i) for i, j in pairs])
    late = pick(range(cut, planes), potential, mass, cells, F32)
    local_map = call(
        functools.partial(combine_kernel, tile_count, planes, side),
        [jax.ShapeDtypeStruct((6 * groups, LANES), F32)],
        [SMEM, SMEM, VMEM, VMEM, VMEM, VMEM, VMEM, VMEM],
    )(tile, lens_weights, cells, first, second, early, late, crossed)[0]
    count = lax.axis_size("depth")
    maps = [local_map]
    maps += [lax.ppermute(local_map, "depth", [(i, i ^ d) for i in range(count)]) for d in range(1, count)]
    return call(
        functools.partial(compose_kernel, count),
        [jax.ShapeDtypeStruct((6 * groups, LANES), F32)],
        [SMEM] + [VMEM] * (count + 1),
        [pltpu.VMEM((count, 6 * groups, LANES), F32)],
    )(depth, *maps, angles)[0].reshape(1, 6, rays)


def solution(mesh):
    return jax.shard_map(
        body,
        mesh=mesh,
        in_specs=(
            P(("depth", "tile"), None, None),
            P(("depth", "tile")),
            P(("depth", "tile")),
            P("depth"),
            P("depth", "tile"),
            P(None, "tile"),
        ),
        out_specs=P("depth", None, "tile"),
        check_vma=False,
    )
```

```python
import functools

import jax
import jax.numpy as jnp
import ml_dtypes
import numpy as np
from jax import lax
from jax.experimental import pallas as pl
from jax.experimental.pallas import tpu as pltpu
from jax.sharding import PartitionSpec as P

F32 = jnp.float32
BF16 = jnp.bfloat16
LANES = 128
VMEM = pl.BlockSpec(memory_space=pltpu.VMEM)
SMEM = pl.BlockSpec(memory_space=pltpu.SMEM)
HBM = pl.BlockSpec(memory_space=pltpu.HBM)


def call(kernel, outs, in_specs, scratch=(), limit=48, flops=0, moved=0):
    return pl.pallas_call(
        kernel,
        out_shape=outs,
        in_specs=in_specs,
        out_specs=jax.tree.map(lambda _: VMEM, outs),
        scratch_shapes=list(scratch),
        compiler_params=pltpu.CompilerParams(vmem_limit_bytes=limit << 20),
        cost_estimate=pl.CostEstimate(flops=flops, bytes_accessed=moved, transcendentals=0),
    )


def mul(a, b):
    return jnp.dot(a, b, preferred_element_type=F32)


def halves(a):
    high = a.astype(BF16)
    return high, (a - high.astype(F32)).astype(BF16)


def label_rows(capacity):
    return -(-capacity // 16) * 16


def tables(side):
    index = np.arange(side, dtype=np.float64) + 1.0
    sines = np.sqrt(2.0 / (side + 1.0)) * np.sin(np.pi * index[:, None] * index[None, :] / (side + 1.0))
    high = sines.astype(np.float32).astype(ml_dtypes.bfloat16)
    low = (sines - high.astype(np.float64)).astype(np.float32).astype(ml_dtypes.bfloat16)
    single = 2.0 - 2.0 * np.cos(np.pi * index / (side + 1.0))
    inverse = -2.0 / (single[:, None] + single[None, :])
    return high, low, inverse.astype(np.float32)


def pack_kernel(tile_count, capacity, layout, tile_ref, owner_ref, place_ref, blocks_ref, *rest):
    outs, slot_ref, count_ref = rest[-2 - len(layout) : -2], rest[-2], rest[-1]
    slots, side = blocks_ref.shape[0], blocks_ref.shape[1]
    spare = tile_count * capacity
    tile = tile_ref[0]
    for x in range(tile_count + 1):
        count_ref[x] = 0
    for i in range(spare):
        slot_ref[i] = -1
    for e in range(slots):
        owner = owner_ref[e]
        live = owner < tile_count
        chunk = jnp.where(live, owner ^ tile, tile_count)
        count = count_ref[chunk]
        count_ref[chunk] = count + 1
        slot_ref[jnp.where(live, chunk * capacity + count, spare + e)] = e
    rows = label_rows(capacity)
    row = lax.broadcasted_iota(jnp.int32, (rows, side), 0)
    for out, members in zip(outs, layout):
        for i, x in enumerate(members):
            base = i * (capacity * side + rows)
            labels = jnp.full((rows, side), -1, jnp.int32)
            for c in range(capacity):
                entry = slot_ref[x * capacity + c]
                safe = jnp.maximum(entry, 0)
                label = jnp.where(entry >= 0, place_ref[safe], -1)
                out[pl.ds(base + c * side, side), :] = blocks_ref[safe]
                labels = jnp.where(row == c, label, labels)
            out[pl.ds(base + capacity * side, rows), :] = labels.astype(F32).astype(BF16)


def solve_kernel(capacity, planes, *refs):
    high_ref, low_ref, inverse_ref = refs[:3]
    chunks, (p_ref, c_ref, edge_ref) = refs[3:-3], refs[-3:]
    side = chunks[0].shape[1]
    for k in range(planes):
        c_ref[k] = jnp.zeros(c_ref.shape[1:], BF16)
    rows = label_rows(capacity)
    for chunk in chunks:
        labels = chunk[pl.ds(capacity * side, rows), :].astype(F32).astype(jnp.int32)
        for c in range(capacity):
            label = labels[c, 0]
            plane = jnp.where(label >= 0, label >> 2, planes)
            top = pl.multiple_of(((label >> 1) & 1) * side, side)
            left = pl.multiple_of((label & 1) * side, side)
            c_ref[plane, pl.ds(top, side), pl.ds(left, side)] = chunk[pl.ds(c * side, side), :]

    high, low, inverse = high_ref[...], low_ref[...], inverse_ref[...]
    across = jnp.concatenate([high, high, low], axis=1)
    down = jnp.concatenate([high, high, low], axis=0)
    pair = jnp.concatenate([high, low], axis=0)

    def right(a, b):
        return mul(jnp.concatenate([a, b, a], axis=1), down)

    def left(a, b):
        return mul(across, jnp.concatenate([a, b, a], axis=0))

    mass = [c_ref[k] for k in range(planes)]
    parts = [halves(mul(jnp.concatenate([m, m], axis=1), pair)) for m in mass]
    parts = [halves(left(*part) * inverse) for part in parts]
    parts = [halves(right(*part)) for part in parts]
    for k in range(planes):
        potential = left(*parts[k])
        p_ref[k] = potential
        for i in range(2 * side // LANES):
            part = potential[:, i * LANES : (i + 1) * LANES]
            edge_ref[pl.ds(2 * i * planes + k, 1), :] = part[:1]
            edge_ref[pl.ds((2 * i + 1) * planes + k, 1), :] = part[2 * side - 1 :]


def shifted(a, axis, step):
    size = a.shape[axis]
    tile = 8 if axis == 0 and size > 8 else min(size, LANES)
    rolled = pltpu.roll(a, (-step) % size, axis)
    at = size - tile if step > 0 else 0
    last = lax.slice_in_dim(rolled, at, at + tile, axis=axis)
    place = lax.broadcasted_iota(jnp.int32, last.shape, axis)
    last = jnp.where(place == (tile - 1 if step > 0 else 0), 0.0, last)
    if size == tile:
        return last
    if step > 0:
        return jnp.concatenate([lax.slice_in_dim(rolled, 0, at, axis=axis), last], axis=axis)
    return jnp.concatenate([last, lax.slice_in_dim(rolled, tile, size, axis=axis)], axis=axis)


def pick_kernel(planes, used, p_ref, c_ref, cells_ref, *refs):
    last_ref, out_ref = refs[-2:]
    start = used[0]
    if len(refs) > 2:
        rest = refs[0][...]
        count = rest.shape[0]
        for i in range(3):
            part = rest.astype(BF16)
            last_ref[pl.ds(out_ref.shape[0] + i * count, count), :] = part
            rest = rest - part.astype(F32)
    side = p_ref.shape[1]
    shift = side.bit_length() - 1
    groups = cells_ref.shape[0] // planes
    width = 2 if groups % 2 == 0 else 1
    sub = lax.broadcasted_iota(jnp.int32, (8, width * LANES), 0)
    column = lax.broadcasted_iota(jnp.int32, (side, width * LANES), 0)
    for k in used:
        p = p_ref[k]
        above, below = shifted(p, 0, -1), shifted(p, 0, 1)
        left, right = shifted(p, 1, -1), shifted(p, 1, 1)
        tilt = 0.5 * (right - left)
        fields = (
            (0.5 * (below - above)).astype(BF16),
            tilt.astype(BF16),
            c_ref[k],
            (0.5 * ((below + above) - (right + left))).astype(BF16),
            (0.5 * (shifted(tilt, 0, 1) - shifted(tilt, 0, -1))).astype(BF16),
        )
        stacked = jnp.concatenate(fields, axis=0)
        for g in range(0, groups, width):
            cells = jnp.concatenate([cells_ref[pl.ds(k * groups + g + w, 1), :] for w in range(width)], axis=1)
            row, col = cells >> shift, cells & (side - 1)
            chosen = (column == col).astype(F32).astype(BF16)
            block, within = row >> 3, sub == (row & 7)
            bits = [(block >> i) & 1 == 1 for i in range((side // 8).bit_length() - 1)]
            every = mul(stacked, chosen)
            for f in range(5):
                picked = every[f * side : (f + 1) * side]
                kept = [picked[v * 8 : v * 8 + 8] for v in range(side // 8)]
                for bit in bits:
                    kept = [jnp.where(bit, b, a) for a, b in zip(kept[::2], kept[1::2])]
                value = jnp.sum(jnp.where(within, kept[0], 0.0), axis=0, keepdims=True)
                for w in range(width):
                    out_ref[pl.ds(((k - start) * 5 + f) * groups + g + w, 1), :] = value[:, w * LANES : (w + 1) * LANES]
    last_ref[pl.ds(0, out_ref.shape[0]), :] = out_ref[...].astype(last_ref.dtype)


def taken(table, index):
    parts = table.shape[1] // LANES
    rows = index.shape[0]
    lane, part = index & (LANES - 1), index >> 7
    out = None
    for i in range(parts):
        spread = jnp.broadcast_to(table[:, i * LANES : (i + 1) * LANES], (rows, LANES))
        got = jnp.take_along_axis(spread, lane, axis=1, mode="promise_in_bounds")
        out = got if out is None else jnp.where(part == i, got, out)
    return out


def edge_kernel(planes, tile_ref, ours_ref, crossed_ref, first_ref, second_ref):
    count = ours_ref.shape[0]
    even = (tile_ref[0] & 1) == 0
    total = ours_ref[...]
    begin = crossed_ref.shape[0] - 3 * count
    for i in range(3):
        total = total + crossed_ref[pl.ds(begin + i * count, count), :].astype(F32)
    for i in range(count // (2 * planes)):
        top = total[2 * i * planes : (2 * i + 1) * planes]
        end = total[(2 * i + 1) * planes : (2 * i + 2) * planes]
        first_ref[pl.ds(i * planes, planes), :] = jnp.where(even, end, top)
        second_ref[pl.ds(i * planes, planes), :] = jnp.where(even, top, end)


def combine_kernel(tile_count, planes, side, tile_ref, weights_ref, cells_ref, first_ref, second_ref, early_ref, late_ref, two_ref, out_ref):
    groups = cells_ref.shape[0] // planes
    shift = side.bit_length() - 1
    tile = tile_ref[0]
    even = (tile & 1) == 0
    starts, ends = tile == 0, tile == tile_count - 1
    axx = ayy = jnp.ones((groups, LANES), F32)
    axy = ayx = bx = by = jnp.zeros((groups, LANES), F32)
    for k in range(planes):
        cells = cells_ref[pl.ds(k * groups, groups), :]
        row, col = cells >> shift, cells & (side - 1)
        first, second = (
            jnp.concatenate([ref[pl.ds(i * planes + k, 1), :] for i in range(side // LANES)], axis=1)
            for ref in (first_ref, second_ref)
        )
        above, below = jnp.where(even, second, first), jnp.where(even, first, second)
        above, below = jnp.where(starts, 0.0, above), jnp.where(ends, 0.0, below)
        at_top, at_end = row == 0, row == side - 1
        up, down = taken(above, col), taken(below, col)
        up_x = taken(shifted(above, 1, 1) - shifted(above, 1, -1), col)
        down_x = taken(shifted(below, 1, 1) - shifted(below, 1, -1), col)
        near = jnp.where(at_top, up, 0.0)
        far = jnp.where(at_end, down, 0.0)
        cross = 0.25 * (jnp.where(at_end, down_x, 0.0) - jnp.where(at_top, up_x, 0.0))

        def read(f):
            early = early_ref.shape[0] // (5 * groups)
            one_ref, j = (early_ref, k) if k < early else (late_ref, k - early)
            other = two_ref[pl.ds((k * 5 + f) * groups, groups), :]
            return one_ref[pl.ds((j * 5 + f) * groups, groups), :] + other.astype(F32)

        weight = weights_ref[k]
        bend_x, bend_y = read(0) + 0.5 * (far - near), read(1)
        extra = 0.5 * (far + near)
        kappa, shear, mixed = read(2) + extra, read(3) + extra, read(4) + cross
        upper, lower = weight * (kappa + shear), weight * (kappa - shear)
        mixed = weight * mixed
        axx, ayx = axx - (upper * axx + mixed * ayx), ayx - (mixed * axx + lower * ayx)
        axy, ayy = axy - (upper * axy + mixed * ayy), ayy - (mixed * axy + lower * ayy)
        bx, by = bx - weight * bend_x, by - weight * bend_y
    for i, value in enumerate((axx, axy, ayx, ayy, bx, by)):
        out_ref[pl.ds(i * groups, groups), :] = value


def compose_kernel(count, depth_ref, *refs):
    angles_ref, out_ref, maps_ref = refs[count:]
    groups = maps_ref.shape[1] // 6
    depth = depth_ref[0]
    for i in range(count):
        maps_ref[depth ^ i] = refs[i][...]

    def part(d, i):
        return maps_ref[d, pl.ds(i * groups, groups), :]

    xx, xy, yx, yy, bx, by = (part(0, i) for i in range(6))
    for d in range(1, count):
        used = d <= depth
        mxx, mxy, myx, myy, mbx, mby = (part(d, i) for i in range(6))
        nxx, nxy = mxx * xx + mxy * yx, mxx * xy + mxy * yy
        nyx, nyy = myx * xx + myy * yx, myx * xy + myy * yy
        new = (nxx, nxy, nyx, nyy, bx + mbx, by + mby)
        xx, xy, yx, yy, bx, by = (jnp.where(used, a, b) for a, b in zip(new, (xx, xy, yx, yy, bx, by)))
    bx = bx + angles_ref[pl.ds(0, groups), :]
    by = by + angles_ref[pl.ds(groups, groups), :]
    for i, value in enumerate((xx, xy, yx, yy, bx, by)):
        out_ref[pl.ds(i * groups, groups), :] = value


def body(density_blocks, block_owner, block_place, lens_weights, ray_cells, ray_angles):
    slots, block_side = density_blocks.shape[:2]
    side = 2 * block_side
    planes, rays = ray_cells.shape
    groups = rays // LANES
    tile_count = lax.axis_size("tile")
    capacity = slots // tile_count
    half = tile_count // 2
    tile = lax.axis_index("tile").astype(jnp.int32).reshape(1)
    depth = lax.axis_index("depth").astype(jnp.int32).reshape(1)
    high, low, inverse = (jnp.asarray(t) for t in tables(side))
    cells = ray_cells.reshape(planes * groups, LANES)
    angles = ray_angles.reshape(2 * groups, LANES)

    def swap(array, bits):
        return lax.ppermute(array, "tile", [(i, i ^ bits) for i in range(tile_count)])

    rows = capacity * block_side + label_rows(capacity)
    order = list(range(2, half)) + [1]
    layout = [[half + x] for x in order] + [[half]] + [[x] for x in order] + [[0]]
    packed = call(
        functools.partial(pack_kernel, tile_count, capacity, layout),
        [jax.ShapeDtypeStruct((rows, block_side), BF16)] * tile_count,
        [SMEM, SMEM, SMEM, VMEM],
        [pltpu.SMEM((tile_count * capacity + slots,), jnp.int32), pltpu.SMEM((tile_count + 1,), jnp.int32)],
        moved=2 * density_blocks.size,
    )(tile, block_owner, block_place, density_blocks)
    theirs = [swap(chunk, x) for x, chunk in zip(order, packed)] + [packed[half - 1]]
    ours = [swap(chunk, x) for x, chunk in zip(order, packed[half:])] + [packed[-1]]
    their_cells = swap(cells, half)

    def solve(arrays):
        return call(
            functools.partial(solve_kernel, capacity, planes),
            [
                jax.ShapeDtypeStruct((planes, side, side), F32),
                jax.ShapeDtypeStruct((planes + 1, side, side), BF16),
                jax.ShapeDtypeStruct((2 * planes * side // LANES, LANES), F32),
            ],
            [VMEM] * (3 + len(arrays)),
        )(high, low, inverse, *arrays)

    def pick(used, potential, mass, at, dtype, *edges):
        count = len(used) * 5 * groups
        return call(
            functools.partial(pick_kernel, planes, used),
            [jax.ShapeDtypeStruct((count + sum(3 * e.shape[0] for e in edges), LANES), dtype)],
            [VMEM] * (3 + len(edges)),
            [pltpu.VMEM((count, LANES), F32)],
            flops=2 * 5 * len(used) * side * side * rays,
        )(potential, mass, at, *edges)[0]

    potential, mass, edges = solve(theirs)
    crossed = swap(pick(range(planes), potential, mass, their_cells, BF16, edges), half)
    potential, mass, edges = solve(ours)
    cut = planes - planes // 4
    early = pick(range(cut), potential, mass, cells, F32)
    crossed, early = lax.optimization_barrier((crossed, early))
    line = jax.ShapeDtypeStruct((planes * side // LANES, LANES), F32)
    first, second = call(functools.partial(edge_kernel, planes), [line, line], [SMEM, VMEM, VMEM])(tile, edges, crossed)
    first = swap(first, 1)
    pairs = [(i, (i + 1) % tile_count) for i in range(1, tile_count, 2)]
    second = lax.ppermute(second, "tile", pairs + [(j, i) for i, j in pairs])
    late = pick(range(cut, planes), potential, mass, cells, F32)
    local_map = call(
        functools.partial(combine_kernel, tile_count, planes, side),
        [jax.ShapeDtypeStruct((6 * groups, LANES), F32)],
        [SMEM, SMEM, VMEM, VMEM, VMEM, VMEM, VMEM, VMEM],
    )(tile, lens_weights, cells, first, second, early, late, crossed)[0]
    count = lax.axis_size("depth")
    maps = [local_map]
    maps += [lax.ppermute(local_map, "depth", [(i, i ^ d) for i in range(count)]) for d in range(1, count)]
    return call(
        functools.partial(compose_kernel, count),
        [jax.ShapeDtypeStruct((6 * groups, LANES), F32)],
        [SMEM] + [VMEM] * (count + 1),
        [pltpu.VMEM((count, 6 * groups, LANES), F32)],
    )(depth, *maps, angles)[0].reshape(1, 6, rays)


def solution(mesh):
    return jax.shard_map(
        body,
        mesh=mesh,
        in_specs=(
            P(("depth", "tile"), None, None),
            P(("depth", "tile")),
            P(("depth", "tile")),
            P("depth"),
            P("depth", "tile"),
            P(None, "tile"),
        ),
        out_specs=P("depth", None, "tile"),
        check_vma=False,
    )
```
